32 devices in a mesh: gx: 2 (over y), gy: 4 (over z), gz: 4 (over x, core).
Axes of the slice: x: 2, y: 2, z: 4, core: 2. Of those that a mesh axis runs over, the one named last changes fastest.
Arguments:
- tensor: float32 [256, 512, 512], P('gx', 'gy', 'gz'), may hold values from -0.75 to 0.75
- factor_a: float32 [256, 256], P(('gy', 'gz'), 'gx'), may hold values from -1.7 to 1.7
- factor_b: float32 [256, 512], P(('gx', 'gz'), 'gy'), may hold values from -1.7 to 1.7
- factor_c: float32 [256, 512], P(('gx', 'gy'), 'gz'), may hold values from -1.7 to 1.7
Outputs:
- grad_a: float32 [256, 256], P(('gy', 'gz'), 'gx')
- grad_b: float32 [256, 512], P(('gx', 'gz'), 'gy')
- grad_c: float32 [256, 512], P(('gx', 'gy'), 'gz')
The draws below stay inside these ranges and needn't reach their ends.
All inputs are finite; a program needn't handle non-finite values.
Results may differ from the reference program's by a relative error of at most 0.00019.
Values sent between devices are 32-bit elements; how exact they have to be, the bound alone decides.
No kernel may reach another device: no remote copies, remote signals or barrier semaphores. Data moves between devices by JAX's collectives and lax.ppermute only.
A program may use at most 128 MiB of HBM per device.

```python
import jax
import jax.numpy as jnp
from jax import lax

R = 64
S = 4
SR = 256
NI = 256
NJ = 512
NK = 512


base_scale = 0.014


def factor_values(key, noise, row_count):
    row_key = jax.random.fold_in(key, 1)
    col_key = jax.random.fold_in(key, 2)
    col_count = noise.shape[0]
    row_scale = jnp.exp(jax.random.uniform(row_key, (row_count,), jnp.float32, -0.5, 0.5) * jnp.log(10.0))
    col_scale = jnp.exp(jax.random.uniform(col_key, (col_count,), jnp.float32, -0.5, 0.5) * jnp.log(10.0))
    rising = 1.0 + 2.0 * jnp.arange(row_count, dtype=jnp.float32) / (row_count - 1)
    return noise * col_scale[:, None] * (row_scale * rising)[None, :] * base_scale


def draw_factor_a(key, part):
    key = jax.random.fold_in(key, 11)
    noise_key = jax.random.fold_in(key, 5)
    noise = jnp.clip(jax.random.normal(noise_key, (SR, NI), jnp.float32), -4.0, 4.0)
    return factor_values(key, noise, NI)


def draw_factor_b(key, part):
    key = jax.random.fold_in(key, 23)
    noise_key = jax.random.fold_in(key, 5)
    noise = jnp.clip(jax.random.normal(noise_key, (SR, NJ), jnp.float32), -4.0, 4.0)
    return factor_values(key, noise, NJ)


def draw_factor_c(key, part):
    key = jax.random.fold_in(key, 37)
    noise_key = jax.random.fold_in(key, 5)
    noise = jnp.clip(jax.random.normal(noise_key, (SR, NK), jnp.float32), -4.0, 4.0)
    return factor_values(key, noise, NK)


def steps_of(key, dims, pieces, low, largest):
    factor_of, own = 1.0, jax.random.fold_in(key, 6)
    for position, parts in pieces:
        heights = jnp.exp(jax.random.uniform(jax.random.fold_in(own, position), (parts,), jnp.float32, low / len(pieces), largest / len(pieces)))
        factor_of = factor_of * jnp.repeat(heights, dims[position] // parts).reshape([-1 if axis == position else 1 for axis in range(len(dims))])
    return factor_of


def centred(rng, dims, scale, limit, shards=(), kind=jnp.bfloat16):
    loudness = steps_of(rng, dims, shards, -0.22, 0.18) if shards else 1.0
    array = jax.random.normal(rng, dims, jnp.float32) * scale * loudness
    return jnp.minimum(jnp.maximum(array, -limit), limit).astype(kind)


def setup_inputs(seed: int = 0) -> dict:
    arg_keys = jax.random.split(jax.random.key(seed), 5)
    return {
        "tensor": centred(arg_keys[0], (NI, NJ, NK), 0.125, 0.75, ((0, 2), (1, 4), (2, 4)), jnp.float32),
        "factor_a": draw_factor_a(jax.random.fold_in(arg_keys[4], 71), 0),
        "factor_b": draw_factor_b(jax.random.fold_in(arg_keys[4], 71), 0),
        "factor_c": draw_factor_c(jax.random.fold_in(arg_keys[4], 71), 0),
    }


exact_mode = lax.Precision.HIGHEST


def block_gram(factor):
    shaped = factor.reshape(S, R, factor.shape[1])
    return jnp.einsum('sri,sti->srt', shaped, shaped, precision=exact_mode)


def scaled_factor(factor, hessian):
    shaped = factor.reshape(S, R, factor.shape[1])
    return jnp.einsum('sri,srt->sti', shaped, hessian, precision=exact_mode).reshape(factor.shape)


def reference(tensor, factor_a, factor_b, factor_c):
    gram_a = block_gram(factor_a)
    gram_b = block_gram(factor_b)
    gram_c = block_gram(factor_c)
    list_a, list_b, list_c = [], [], []
    for start in range(S):
        part_a = factor_a[start * R:(start + 1) * R]
        part_b = factor_b[start * R:(start + 1) * R]
        part_c = factor_c[start * R:(start + 1) * R]
        first_y = jnp.einsum('ijk,cj->cik', tensor, part_b, precision=exact_mode)
        list_a.append(jnp.einsum('cik,ck->ci', first_y, part_c, precision=exact_mode))
        list_c.append(jnp.einsum('cik,ci->ck', first_y, part_a, precision=exact_mode))
        second_y = jnp.einsum('ijk,ck->cij', tensor, part_c, precision=exact_mode)
        list_b.append(jnp.einsum('cij,ci->cj', second_y, part_a, precision=exact_mode))
    m_a = jnp.concatenate(list_a, axis=0)
    m_b = jnp.concatenate(list_b, axis=0)
    m_c = jnp.concatenate(list_c, axis=0)
    grad_a = scaled_factor(factor_a, gram_b * gram_c) - m_a
    grad_b = scaled_factor(factor_b, gram_a * gram_c) - m_b
    grad_c = scaled_factor(factor_c, gram_a * gram_b) - m_c
    return (grad_a, grad_b, grad_c)
```

```python
import jax
import jax.numpy as jnp
from jax import lax
from jax.experimental import pallas as pl
from jax.experimental.pallas import tpu as pltpu
from jax.sharding import PartitionSpec as P

R = 64
PAIR = 2 * R
GROUP = 8
UNROLL = 8
BUFFERS = 4
TILE = 8
TURNS = 16
MIB = 1024 * 1024


def split(value):
    high = value.astype(jnp.bfloat16)
    low = (value - high.astype(jnp.float32)).astype(jnp.bfloat16)
    return high, low


def pair_grams(rows):
    row = lax.broadcasted_iota(jnp.int32, (PAIR, PAIR), 0) // R
    col = lax.broadcasted_iota(jnp.int32, (PAIR, PAIR), 1) // R
    blocks = []
    for pair in range(rows.shape[0] // PAIR):
        part = rows[pair * PAIR : (pair + 1) * PAIR, :]
        high, low = split(part)
        gram = lax.dot_general(
            jnp.concatenate([high, low, high], axis=1),
            jnp.concatenate([high, high, low], axis=1),
            (((1,), (1,)), ((), ())),
            preferred_element_type=jnp.float32,
        )
        blocks.append(folded(jnp.where(row == col, gram, 0.0)))
    return jnp.concatenate(blocks, axis=0)


def folded(value):
    half = value.shape[1] // 2
    return value + jnp.concatenate([value[:, half:], value[:, :half]], axis=1)


def packs(rows):
    return rows % 16 == 0


def packed_rows(rows):
    return rows // 2 if packs(rows) else rows


def packed(gram, rows):
    blocks = gram.reshape(-1, rows, gram.shape[1])
    if not packs(rows):
        return blocks
    half = rows // 2
    lane = lax.broadcasted_iota(jnp.int32, (blocks.shape[0], half, gram.shape[1]), 2)
    return jnp.where(lane < R, blocks[:, :half], blocks[:, half:])


def unpacked(block, rows):
    if not packs(rows):
        return block
    lane = lax.broadcasted_iota(jnp.int32, block.shape, 1)
    return folded(jnp.concatenate([jnp.where(lane < R, block, 0.0), jnp.where(lane < R, 0.0, block)], axis=0))


def here():
    return lax.axis_index("gx"), lax.axis_index("gy"), lax.axis_index("gz")


def take(refs, *counts):
    groups, first = [], 0
    for count in counts:
        groups.append(refs[first : first + count])
        first += count
    return groups, refs[first:]


def put(ref, values):
    first = 0
    for value in values:
        ref[first : first + value.shape[0], :] = value
        first += value.shape[0]


def total_of(refs):
    total = refs[0][...]
    for ref in refs[1:]:
        total = total + ref[...]
    return total


def own_kernel(sizes, a_ref, b_ref, c_ref, ac_ref, own_b, sems):
    ra = a_ref.shape[0]
    targets = [ac_ref.at[:ra], own_b, ac_ref.at[ra:]]
    copies = [
        pltpu.make_async_copy(source, target, sems.at[n])
        for n, (source, target) in enumerate(zip([a_ref, b_ref, c_ref], targets))
    ]
    for copy in copies:
        copy.start()
    for copy in copies:
        copy.wait()


def pack_kernel(sizes, *refs):
    nx, ny, nz, ra, rb, rc = sizes
    (ac, (b, for_z, for_x)), _ = take(refs, ny, 3)
    put(for_z, [ref[:ra, :] for ref in ac] + [b[...]])
    put(for_x, [ref[ra:, :] for ref in ac])


def sweep(blocks, contract, reduce, results):
    @pl.loop(0, blocks // UNROLL)
    def _(turn):
        for n in range(UNROLL + 1):
            if n < UNROLL:
                contract(turn, n, results[n % BUFFERS])
            if n:
                reduce(turn, n - 1, results[(n - 1) % BUFFERS])


def spread(counts, turn, n):
    turns = sum(counts) // (GROUP * UNROLL)
    first = 0
    for array, count in enumerate(counts):
        share = count // (GROUP * turns)
        if n < share:
            start = (turn * share + n) * GROUP
            return array, pl.multiple_of(start, GROUP), pl.multiple_of(first + start, GROUP)
        n -= share
        first += count


def weights(columns):
    both = jnp.concatenate(split(columns), axis=1)
    return jnp.concatenate([both, both], axis=0)


def product(pair, weights):
    value = jnp.dot(pair, weights, preferred_element_type=jnp.float32)
    half = value.shape[1] // 2
    return value[:, :half] + value[:, half:]


def accurate(rows, columns):
    return product(jnp.concatenate(split(rows), axis=1), weights(columns))


def flat(block):
    return block.reshape(block.shape[0] * block.shape[1], block.shape[2])


def transpose(pairs, first, turned, start, count):
    for n in range(count):
        turned[start + n] = transposed(pairs[first + n])


def transposed(pair):
    half = pair.shape[1] // 2
    return jnp.concatenate([pair[:, :half].T, pair[:, half:].T], axis=1)


def tensor_kernel(sizes, *refs):
    (b, (tensor, pairs, turned, rows_b)), _ = take(refs, sizes[0], 4)
    put(rows_b, [ref[...] for ref in b])

    @pl.loop(0, tensor.shape[0] // (2 * TURNS))
    def _(turn):
        for n in range(2 * TURNS):
            place = turn * 2 * TURNS + n
            pair = jnp.concatenate(split(tensor[place]), axis=1)
            pairs[place] = pair
        for n in range(TURNS):
            transpose(pairs, turn * TURNS + n, turned, turn * TURNS + n, 1)


def own_half(x, nx):
    return x // (nx // 2)


def early_columns(sizes, packs_x, c_ref):
    nx, ny, nz, ra, rb, rc = sizes
    x, y, z = here()
    part = lax.rem(x, nx // 2)
    for sx in range(nx // 2):
        for sy in range(ny):
            place = ((part ^ sx) * ny + (y ^ sy)) * rc
            c_ref[pl.ds(place, rc), :] = packs_x[sx][sy * rc : (sy + 1) * rc, :]


def early_loop(first, count, pairs, weights_ref, own_y, turned):
    nj = pairs.shape[1]
    turns = GROUP // 2
    start = pairs.shape[0] // 2 + first // 2
    for block in range(count // GROUP):
        own_y[pl.ds(block * GROUP * nj, GROUP * nj), :] = product(
            flat(pairs[pl.ds(first + block * GROUP, GROUP)]), weights_ref[...]
        )
        transpose(pairs, start + block * turns, turned, block * turns, turns)


def early_kernel(sizes, *refs):
    (packs_x, (pairs, own_y, turned, c_ref, cc_ref)), _ = take(refs, sizes[0] // 2, 5)
    early_columns(sizes, packs_x, c_ref)
    cc_ref[...] = weights(c_ref[...].T)
    early_loop(0, own_y.shape[0] // pairs.shape[1], pairs, cc_ref, own_y, turned)


def later_kernel(sizes, pairs, cc_ref, own_y, turned):
    count = own_y.shape[0] // pairs.shape[1]
    early_loop(pairs.shape[0] - count, count, pairs, cc_ref, own_y, turned)


def stack_kernel(sizes, *refs):
    *values, _, target = refs
    put(target, [value[...] for value in values])


def first_kernel(sizes, *refs):
    nx, ny, nz, ra, rb, rc = sizes
    (packs_z, packs_x, own_y, (own_c, pairs), sends), refs = take(refs, 2, nx // 2, 2, 2, 2)
    a_ref, at_ref, b_ref, c_ref, bt_ref, cc_ref, ma_ref, mb_ref = refs[:8]
    (ca_ref, cb_ref), results, (rows_of,) = refs[8:10], refs[10:-1], refs[-1:]
    pa, pb = packed_rows(ra), packed_rows(rb)
    x, y, z = here()
    ni, nj = pairs.shape[0], pairs.shape[1]
    lanes = c_ref.shape[0] // 2
    half = own_half(x, nx)
    own, other = half * lanes, (1 - half) * lanes

    for sz in range(nz):
        start = sz // 2 * (ny * ra + nx * rb)
        for sy in range(ny):
            a_ref[pl.ds(((y ^ sy) * nz + (z ^ sz)) * ra, ra), :] = packs_z[sz % 2][start : start + ra, :]
            start += ra
        for sx in range(nx):
            b_ref[pl.ds(((x ^ sx) * nz + (z ^ sz)) * rb, rb), :] = packs_z[sz % 2][start : start + rb, :]
            start += rb
    c_ref[pl.ds(own, lanes), :] = own_c[...]
    for sx in range(nx // 2):
        for sy in range(ny):
            place = ((x ^ (sx + nx // 2)) * ny + (y ^ sy)) * rc
            c_ref[pl.ds(place, rc), :] = packs_x[sx][sy * rc : (sy + 1) * rc, :]
    for n, first in enumerate((own, other)):
        at_ref[n] = a_ref[pl.ds(first, lanes), :].T
        bt_ref[n] = b_ref[pl.ds(first, lanes), :].T
    cc_ref[...] = weights(c_ref[pl.ds(other, lanes), :].T)
    gram = pair_grams(c_ref[...])
    ca_ref[...] = packed(gram, ra)
    cb_ref[...] = packed(gram, rb)
    mb_ref[...] = jnp.zeros_like(mb_ref)

    counts = [ref.shape[0] // nj for ref in own_y]

    def contract(turn, n, result):
        slices = spread(counts, turn, n)[2]
        result[...] = product(flat(pairs[pl.ds(slices, GROUP)]), cc_ref[...])

    def reduce(turn, n, result):
        part, start, first = spread(counts, turn, n)
        start = pl.multiple_of(start * nj, GROUP * nj)
        for n in range(2):
            scales = [jnp.broadcast_to(at_ref[n, pl.ds(first + g, 1), :], (TILE, lanes)) for g in range(GROUP)]
            sums = [jnp.zeros((TILE, lanes), jnp.float32)] * GROUP
            for tile in range(nj // TILE):
                rows = slice(tile * TILE, (tile + 1) * TILE)
                total = mb_ref[n, rows, :]
                across = bt_ref[n, rows, :]
                for g in range(GROUP):
                    place = g * nj + tile * TILE
                    if n == 0:
                        value = own_y[part][pl.ds(start + place, TILE), :]
                    else:
                        value = result[place : place + TILE, :]
                    total = total + scales[g] * value
                    sums[g] = sums[g] + across * value
                mb_ref[n, rows, :] = total
            for g in range(GROUP):
                ma_ref[n, pl.ds(first + g, 1), :] = jnp.sum(sums[g], axis=0, keepdims=True)

    sweep(ni // GROUP, contract, reduce, results)

    for n in range(2):
        rows_of[0, n * lanes : (n + 1) * lanes, :] = ma_ref[n].T
        rows_of[1, n * lanes : (n + 1) * lanes, :] = mb_ref[n].T
    for sz in range(nz):
        to_z = z ^ sz
        count = ny * ra + nx * rb + pa + pb
        put(
            sends[sz % 2].at[sz // 2 * count : (sz // 2 + 1) * count],
            [rows_of[0, pl.ds((((y ^ sy) * nz + to_z) * ra) ^ own, ra), :] for sy in range(ny)]
            + [rows_of[1, pl.ds((((x ^ sx) * nz + to_z) * rb) ^ own, rb), :] for sx in range(nx)]
            + [ca_ref[y * nz + to_z], cb_ref[x * nz + to_z]],
        )


def third_loop(turned, columns, weights_ref, result_refs, total_ref):
    total_ref[...] = jnp.zeros_like(total_ref)
    nk, lanes = total_ref.shape
    counts = [ref.shape[0] for ref in turned]

    def contract(turn, n, result):
        array, start, _ = spread(counts, turn, n)
        result[...] = product(flat(turned[array][pl.ds(start, GROUP)]), weights_ref[...])

    def reduce(turn, n, result):
        first = spread(counts, turn, n)[2]
        scales = [jnp.broadcast_to(columns[pl.ds(first + g, 1), :], (TILE, lanes)) for g in range(GROUP)]
        for tile in range(nk // TILE):
            rows = slice(tile * TILE, (tile + 1) * TILE)
            total = total_ref[rows, :]
            for g in range(GROUP):
                place = g * nk + tile * TILE
                total = total + scales[g] * result[place : place + TILE, :]
            total_ref[rows, :] = total

    sweep(sum(counts) // GROUP, contract, reduce, result_refs)


def partner_kernel(sizes, *refs):
    nx, ny, nz, ra, rb, rc = sizes
    (turned, (a_ref, at_ref, b_ref), sends), refs = take(refs, 3, 3, nx // 2)
    (kept_b, tb_ref, tc_ref, bb_ref, mc_ref, ba_ref, bc_ref), results, rows_of = refs[:7], refs[7:-1], refs[-1]
    x, y, z = here()
    lanes = mc_ref.shape[1]
    other = (1 - own_half(x, nx)) * lanes
    bb_ref[...] = weights(b_ref[pl.ds(other, lanes), :].T)
    gram = pair_grams(a_ref[...])
    tb_ref[...] = packed(gram, rb)
    tc_ref[...] = packed(gram, rc)
    gram = pair_grams(b_ref[...])
    ba_ref[...] = packed(gram, ra)
    bc_ref[...] = packed(gram, rc)
    third_loop(turned, at_ref.at[1], bb_ref, results, mc_ref)
    rows_of[...] = mc_ref[...].T
    for sx in range(nx // 2):
        to_x = x ^ (sx + nx // 2)
        put(
            sends[sx],
            [rows_of[pl.ds((to_x * ny + (y ^ sy)) * rc - other, rc), :] for sy in range(ny)]
            + [tb_ref[to_x * nz + z], tc_ref[to_x * ny + y]],
        )
    grams = []
    for sy in range(ny):
        grams += [ba_ref[(y ^ sy) * nz + z], bc_ref[x * ny + (y ^ sy)]]
    put(kept_b, grams)


def own_third_kernel(sizes, *refs):
    nx, ny, nz, ra, rb, rc = sizes
    (turned, (at_ref, b_ref, tb_ref, tc_ref), sends), refs = take(refs, 3, 4, nx // 2)
    (bb_ref, mc_ref), results, rows_of = refs[:2], refs[2:-1], refs[-1]
    x, y, z = here()
    lanes = mc_ref.shape[1]
    own = own_half(x, nx) * lanes
    bb_ref[...] = weights(b_ref[pl.ds(own, lanes), :].T)
    third_loop(turned, at_ref.at[0], bb_ref, results, mc_ref)
    rows_of[...] = mc_ref[...].T
    for sx in range(nx // 2):
        to_x = x ^ sx
        put(
            sends[sx],
            [rows_of[pl.ds((to_x * ny + (y ^ sy)) * rc - own, rc), :] for sy in range(ny)]
            + [tb_ref[to_x * nz + z], tc_ref[to_x * ny + y]],
        )


def core_kernel(sizes, own, other, *outs):
    count = outs[0].shape[0]
    for part, out in enumerate(outs):
        rows = slice(part * count, (part + 1) * count)
        out[...] = own[rows, :] + other[rows, :]


def middle_kernel(sizes, *refs):
    nx, ny, nz, ra, rb, rc = sizes
    (from_z, from_x, (grams_b,), for_y, for_x), (kept,) = take(refs, nz // 2, nx, 1, ny, nx)
    pa, pb, pc = packed_rows(ra), packed_rows(rb), packed_rows(rc)
    sum_z, sum_x = total_of(from_z), total_of(from_x)
    for sy in range(ny):
        put(
            for_y[sy],
            [
                sum_z[sy * ra : (sy + 1) * ra],
                sum_x[sy * rc : (sy + 1) * rc],
                grams_b[sy * (pa + pc) : (sy + 1) * (pa + pc), :],
            ],
        )
    for sx in range(nx):
        for_x[sx][...] = sum_z[ny * ra + sx * rb : ny * ra + (sx + 1) * rb]
    put(kept, [sum_z[ny * ra + nx * rb :], sum_x[ny * rc :]])


def scaled(one, other, rows, factor_ref, first_row):
    hessian = unpacked(one * other, rows)
    lane = lax.broadcasted_iota(jnp.int32, hessian.shape, 1)
    hessian = jnp.where(lane // R == lax.rem(first_row // R, 2), hessian, 0.0)
    pair = pl.multiple_of(first_row // PAIR * PAIR, PAIR)
    return accurate(hessian, factor_ref[pl.ds(pair, PAIR), :])


def grad_b_kernel(sizes, *refs):
    nx, ny, nz, ra, rb, rc = sizes
    (from_x, (kept, b_ref, grad_b)), _ = take(refs, nx, 3)
    pa, pb = packed_rows(ra), packed_rows(rb)
    x, y, z = here()
    gram_cb, gram_ab = kept[pa : pa + pb, :], kept[pa + pb : pa + 2 * pb, :]
    grad_b[...] = scaled(gram_ab, gram_cb, rb, b_ref, (x * nz + z) * rb) - total_of(from_x)


def last_kernel(sizes, *refs):
    nx, ny, nz, ra, rb, rc = sizes
    (from_y, (kept, a_ref, c_ref, grad_a, grad_c)), _ = take(refs, ny, 5)
    pa, pb = packed_rows(ra), packed_rows(rb)
    x, y, z = here()
    sum_y = total_of(from_y)
    m_a, m_c = sum_y[:ra], sum_y[ra : ra + rc]
    gram_ba, gram_bc = sum_y[ra + rc : ra + rc + pa], sum_y[ra + rc + pa :]
    gram_ca, gram_ac = kept[:pa, :], kept[pa + 2 * pb :, :]
    grad_a[...] = scaled(gram_ba, gram_ca, ra, a_ref, (y * nz + z) * ra) - m_a
    grad_c[...] = scaled(gram_ac, gram_bc, rc, c_ref, (x * ny + y) * rc) - m_c


def swap(value, axis, distance):
    return lax.ppermute(value, axis, [(i, i ^ distance) for i in range(lax.axis_size(axis))])


def partners(values, axis, stride=1):
    count = lax.axis_size(axis) // stride
    if not isinstance(values, (list, tuple)):
        values = [values] * count
    return [values[0]] + [swap(values[s], axis, s * stride) for s in range(1, count)]


def swapped(value):
    return swap(value, "gz", 1)


def body(tensor, factor_a, factor_b, factor_c):
    nx, ny, nz = (lax.axis_size(name) for name in ("gx", "gy", "gz"))
    ra, rb, rc = factor_a.shape[0], factor_b.shape[0], factor_c.shape[0]
    pa, pb, pc = packed_rows(ra), packed_rows(rb), packed_rows(rc)
    lanes = factor_a.shape[1]
    total = ra * ny * nz
    sizes = (nx, ny, nz, ra, rb, rc)
    message = ny * ra + nx * rb + pa + pb
    f32, bf16 = jnp.float32, jnp.bfloat16
    vmem = pl.BlockSpec(memory_space=pltpu.VMEM)
    tensor = pltpu.with_memory_space_constraint(tensor, pltpu.VMEM)
    flops = 2 * 3 * tensor.size * total

    def rows(count):
        return jax.ShapeDtypeStruct((count, lanes), f32)

    def call(kernel, outs, args, scratch=(), limit=4, cost=None, space=pltpu.VMEM):
        return pl.pallas_call(
            lambda *refs: kernel(sizes, *refs),
            out_shape=outs,
            in_specs=[pl.BlockSpec(memory_space=space)] * len(args),
            out_specs=[vmem] * len(outs),
            scratch_shapes=scratch,
            compiler_params=pltpu.CompilerParams(vmem_limit_bytes=limit * MIB),
            cost_estimate=cost,
            name=kernel.__name__,
        )(*args)

    work = pl.CostEstimate(flops=flops, bytes_accessed=4 * tensor.size, transcendentals=0)

    ni, nj, nk = tensor.shape
    half = total // 2
    results = [pltpu.VMEM((GROUP * nj, half), f32)] * BUFFERS
    weight = pltpu.VMEM((2 * lanes, 2 * half), bf16)
    halves = pltpu.VMEM((2, lanes, half), f32)
    later = ni // 2

    def own_part(count):
        return pltpu.VMEM((count * nj, half), f32)

    def slices(count):
        return pltpu.VMEM((count, nk, 2 * nj), bf16)

    def gram_blocks(count):
        return pltpu.VMEM((total // count, packed_rows(count), PAIR), f32)

    def array(ref):
        return jax.ShapeDtypeStruct(ref.shape, ref.dtype)

    own_ac, own_b = call(
        own_kernel,
        [rows(ra + rc), rows(rb)],
        [pltpu.with_memory_space_constraint(value, pltpu.HBM) for value in (factor_a, factor_b, factor_c)],
        [pltpu.SemaphoreType.DMA((3,))],
        cost=work,
        space=pltpu.HBM,
    )
    ac = partners(own_ac, "gy")
    b = partners(own_b, "gx")
    pairs, turned_0, rows_b = call(
        tensor_kernel, [slices(ni), slices(ni // 2), rows(nx * rb)], [*b, tensor], (), 8, work
    )
    for_z, for_x = call(pack_kernel, [rows(ny * ra + nx * rb), rows(ny * rc)], [*ac, rows_b])
    from_x = partners(for_x, "gx")
    by_x = partners(for_z, "gz", 2)
    own_y_0, turned_1, own_c, weights_c = call(
        early_kernel,
        [own_part(ni - later), slices((ni - later) // 2), rows(half), array(weight)],
        [*from_x[: nx // 2], pairs],
        (),
        8,
        work,
    )
    (stack,) = call(stack_kernel, [rows(nz // 2 * (ny * ra + nx * rb))], [*by_x, own_c])
    from_z = [stack, swapped(stack)]
    own_y_1, turned_2 = call(later_kernel, [own_part(later), slices(later // 2)], [pairs, weights_c], (), 8, work)
    turned = [turned_0, turned_1, turned_2]
    own_core, other_core, block_a, columns_a, block_b, block_c = call(
        first_kernel,
        [rows(nz // 2 * message)] * 2 + [rows(total), array(halves), rows(total), rows(total)],
        [*from_z, *from_x[nx // 2 :], own_y_0, own_y_1, own_c, pairs],
        [
            halves, weight, halves, halves, gram_blocks(ra), gram_blocks(rb),
            *results, pltpu.VMEM((2, total, lanes), f32),
        ],
        12,
        work,
    )
    other_core = swapped(other_core)
    outs = call(
        partner_kernel,
        [rows(ny * rc + pb + pc)] * (nx // 2)
        + [rows(ny * (pa + pc)), array(gram_blocks(rb)), array(gram_blocks(rc))],
        [*turned, block_a, columns_a, block_b],
        [
            weight, pltpu.VMEM((nk, half), f32), gram_blocks(ra), gram_blocks(rc),
            *results, pltpu.VMEM((half, lanes), f32),
        ],
        8,
        work,
    )
    sums_x, (grams_b, grams_ab, grams_ac) = outs[: nx // 2], outs[nx // 2 :]
    sums_x = [swap(value, "gx", s + nx // 2) for s, value in enumerate(sums_x)]
    sums_z = call(core_kernel, [rows(message)] * (nz // 2), [own_core, other_core])
    sums_z = partners(sums_z, "gz", 2)
    own_x = call(
        own_third_kernel,
        [rows(ny * rc + pb + pc)] * (nx // 2),
        [*turned, columns_a, block_b, grams_ab, grams_ac],
        [weight, pltpu.VMEM((nk, half), f32), *results, pltpu.VMEM((half, lanes), f32)],
        8,
        work,
    )
    sums_x = [swap(value, "gx", s) if s else value for s, value in enumerate(own_x)] + sums_x
    outs = call(
        middle_kernel,
        [rows(ra + rc + pa + pc)] * ny + [rows(rb)] * nx + [rows(pa + pb + pb + pc)],
        [*sums_z, *sums_x, grams_b],
    )
    sums_y, sums_x, kept = outs[:ny], outs[ny : ny + nx], outs[ny + nx]
    sums_y = partners(sums_y, "gy")
    sums_x = partners(sums_x, "gx")
    (grad_b,) = call(grad_b_kernel, [rows(rb)], [*sums_x, kept, block_b], cost=work)
    grad_a, grad_c = call(last_kernel, [rows(ra), rows(rc)], [*sums_y[::-1], kept, block_a, block_c])
    return grad_a, grad_b, grad_c


def solution(mesh):
    in_specs = (
        P("gx", "gy", "gz"),
        P(("gy", "gz"), "gx"),
        P(("gx", "gz"), "gy"),
        P(("gx", "gy"), "gz"),
    )
    out_specs = (P(("gy", "gz"), "gx"), P(("gx", "gz"), "gy"), P(("gx", "gy"), "gz"))
    return jax.shard_map(body, mesh=mesh, in_specs=in_specs, out_specs=out_specs, check_vma=False)
```

```python
import jax
import jax.numpy as jnp
from jax import lax
from jax.experimental import pallas as pl
from jax.experimental.pallas import tpu as pltpu
from jax.sharding import PartitionSpec as P

R = 64
PAIR = 2 * R
GROUP = 8
UNROLL = 16
BUFFERS = 4
TILE = 8
TURNS = 16
MIB = 1024 * 1024


def split(value):
    high = value.astype(jnp.bfloat16)
    low = (value - high.astype(jnp.float32)).astype(jnp.bfloat16)
    return high, low


def pair_grams(rows):
    row = lax.broadcasted_iota(jnp.int32, (PAIR, PAIR), 0) // R
    col = lax.broadcasted_iota(jnp.int32, (PAIR, PAIR), 1) // R
    blocks = []
    for pair in range(rows.shape[0] // PAIR):
        part = rows[pair * PAIR : (pair + 1) * PAIR, :]
        high, low = split(part)
        gram = lax.dot_general(
            jnp.concatenate([high, low, high], axis=1),
            jnp.concatenate([high, high, low], axis=1),
            (((1,), (1,)), ((), ())),
            preferred_element_type=jnp.float32,
        )
        blocks.append(folded(jnp.where(row == col, gram, 0.0)))
    return jnp.concatenate(blocks, axis=0)


def folded(value):
    half = value.shape[1] // 2
    return value + jnp.concatenate([value[:, half:], value[:, :half]], axis=1)


def packs(rows):
    return rows % 16 == 0


def packed_rows(rows):
    return rows // 2 if packs(rows) else rows


def packed(gram, rows):
    blocks = gram.reshape(-1, rows, gram.shape[1])
    if not packs(rows):
        return blocks
    half = rows // 2
    lane = lax.broadcasted_iota(jnp.int32, (blocks.shape[0], half, gram.shape[1]), 2)
    return jnp.where(lane < R, blocks[:, :half], blocks[:, half:])


def unpacked(block, rows):
    if not packs(rows):
        return block
    lane = lax.broadcasted_iota(jnp.int32, block.shape, 1)
    return folded(jnp.concatenate([jnp.where(lane < R, block, 0.0), jnp.where(lane < R, 0.0, block)], axis=0))


def here():
    return lax.axis_index("gx"), lax.axis_index("gy"), lax.axis_index("gz")


def take(refs, *counts):
    groups, first = [], 0
    for count in counts:
        groups.append(refs[first : first + count])
        first += count
    return groups, refs[first:]


def put(ref, values):
    first = 0
    for value in values:
        ref[first : first + value.shape[0], :] = value
        first += value.shape[0]


def total_of(refs):
    total = refs[0][...]
    for ref in refs[1:]:
        total = total + ref[...]
    return total


def own_kernel(sizes, a_ref, b_ref, c_ref, ac_ref, own_b, sems):
    ra = a_ref.shape[0]
    targets = [ac_ref.at[:ra], own_b, ac_ref.at[ra:]]
    copies = [
        pltpu.make_async_copy(source, target, sems.at[n])
        for n, (source, target) in enumerate(zip([a_ref, b_ref, c_ref], targets))
    ]
    for copy in copies:
        copy.start()
    for copy in copies:
        copy.wait()


def pack_kernel(sizes, *refs):
    nx, ny, nz, ra, rb, rc = sizes
    (ac, (b, for_z, for_x)), _ = take(refs, ny, 3)
    put(for_z, [ref[:ra, :] for ref in ac] + [b[...]])
    put(for_x, [ref[ra:, :] for ref in ac])


def sweep(blocks, contract, reduce, results):
    @pl.loop(0, blocks // UNROLL)
    def _(turn):
        for n in range(UNROLL + 1):
            if n < UNROLL:
                contract(turn, n, results[n % BUFFERS])
            if n:
                reduce(turn, n - 1, results[(n - 1) % BUFFERS])


def spread(counts, turn, n):
    turns = sum(counts) // (GROUP * UNROLL)
    first = 0
    for array, count in enumerate(counts):
        share = count // (GROUP * turns)
        if n < share:
            start = (turn * share + n) * GROUP
            return array, pl.multiple_of(start, GROUP), pl.multiple_of(first + start, GROUP)
        n -= share
        first += count


def weights(columns):
    both = jnp.concatenate(split(columns), axis=1)
    return jnp.concatenate([both, both], axis=0)


def product(pair, weights):
    value = jnp.dot(pair, weights, preferred_element_type=jnp.float32)
    half = value.shape[1] // 2
    return value[:, :half] + value[:, half:]


def accurate(rows, columns):
    return product(jnp.concatenate(split(rows), axis=1), weights(columns))


def flat(block):
    return block.reshape(block.shape[0] * block.shape[1], block.shape[2])


def transpose(pairs, first, turned, start, count):
    for n in range(count):
        turned[start + n] = transposed(pairs[first + n])


def transposed(pair):
    half = pair.shape[1] // 2
    return jnp.concatenate([pair[:, :half].T, pair[:, half:].T], axis=1)


def tensor_kernel(sizes, *refs):
    (b, (tensor, pairs, turned, rows_b)), _ = take(refs, sizes[0], 4)
    put(rows_b, [ref[...] for ref in b])

    @pl.loop(0, tensor.shape[0] // (2 * TURNS))
    def _(turn):
        for n in range(2 * TURNS):
            place = turn * 2 * TURNS + n
            pair = jnp.concatenate(split(tensor[place]), axis=1)
            pairs[place] = pair
        for n in range(TURNS):
            transpose(pairs, turn * TURNS + n, turned, turn * TURNS + n, 1)


def own_half(x, nx):
    return x // (nx // 2)


def early_columns(sizes, packs_x, c_ref):
    nx, ny, nz, ra, rb, rc = sizes
    x, y, z = here()
    part = lax.rem(x, nx // 2)
    for sx in range(nx // 2):
        for sy in range(ny):
            place = ((part ^ sx) * ny + (y ^ sy)) * rc
            c_ref[pl.ds(place, rc), :] = packs_x[sx][sy * rc : (sy + 1) * rc, :]


def early_loop(first, count, pairs, weights_ref, own_y, turned):
    nj = pairs.shape[1]
    turns = GROUP // 2
    start = pairs.shape[0] // 2 + first // 2
    for block in range(count // GROUP):
        own_y[pl.ds(block * GROUP * nj, GROUP * nj), :] = product(
            flat(pairs[pl.ds(first + block * GROUP, GROUP)]), weights_ref[...]
        )
        transpose(pairs, start + block * turns, turned, block * turns, turns)


def early_kernel(sizes, *refs):
    (packs_x, (pairs, own_y, turned, c_ref, cc_ref)), _ = take(refs, sizes[0] // 2, 5)
    early_columns(sizes, packs_x, c_ref)
    cc_ref[...] = weights(c_ref[...].T)
    early_loop(0, own_y.shape[0] // pairs.shape[1], pairs, cc_ref, own_y, turned)


def later_kernel(sizes, pairs, cc_ref, own_y, turned):
    count = own_y.shape[0] // pairs.shape[1]
    early_loop(pairs.shape[0] - count, count, pairs, cc_ref, own_y, turned)


def stack_kernel(sizes, *refs):
    *values, _, target = refs
    put(target, [value[...] for value in values])


def first_kernel(sizes, *refs):
    nx, ny, nz, ra, rb, rc = sizes
    (packs_z, packs_x, own_y, (own_c, pairs), sends), refs = take(refs, 2, nx // 2, 2, 2, 2)
    a_ref, at_ref, b_ref, c_ref, bt_ref, cc_ref, ma_ref, mb_ref = refs[:8]
    (ca_ref, cb_ref), results, (rows_of,) = refs[8:10], refs[10:-1], refs[-1:]
    pa, pb = packed_rows(ra), packed_rows(rb)
    x, y, z = here()
    ni, nj = pairs.shape[0], pairs.shape[1]
    lanes = c_ref.shape[0] // 2
    half = own_half(x, nx)
    own, other = half * lanes, (1 - half) * lanes

    for sz in range(nz):
        start = sz // 2 * (ny * ra + nx * rb)
        for sy in range(ny):
            a_ref[pl.ds(((y ^ sy) * nz + (z ^ sz)) * ra, ra), :] = packs_z[sz % 2][start : start + ra, :]
            start += ra
        for sx in range(nx):
            b_ref[pl.ds(((x ^ sx) * nz + (z ^ sz)) * rb, rb), :] = packs_z[sz % 2][start : start + rb, :]
            start += rb
    c_ref[pl.ds(own, lanes), :] = own_c[...]
    for sx in range(nx // 2):
        for sy in range(ny):
            place = ((x ^ (sx + nx // 2)) * ny + (y ^ sy)) * rc
            c_ref[pl.ds(place, rc), :] = packs_x[sx][sy * rc : (sy + 1) * rc, :]
    for n, first in enumerate((own, other)):
        at_ref[n] = a_ref[pl.ds(first, lanes), :].T
        bt_ref[n] = b_ref[pl.ds(first, lanes), :].T
    cc_ref[...] = weights(c_ref[pl.ds(other, lanes), :].T)
    gram = pair_grams(c_ref[...])
    ca_ref[...] = packed(gram, ra)
    cb_ref[...] = packed(gram, rb)
    mb_ref[...] = jnp.zeros_like(mb_ref)

    counts = [ref.shape[0] // nj for ref in own_y]

    def contract(turn, n, result):
        slices = spread(counts, turn, n)[2]
        result[...] = product(flat(pairs[pl.ds(slices, GROUP)]), cc_ref[...])

    def reduce(turn, n, result):
        part, start, first = spread(counts, turn, n)
        start = pl.multiple_of(start * nj, GROUP * nj)
        for n in range(2):
            scales = [jnp.broadcast_to(at_ref[n, pl.ds(first + g, 1), :], (TILE, lanes)) for g in range(GROUP)]
            sums = [jnp.zeros((TILE, lanes), jnp.float32)] * GROUP
            for tile in range(nj // TILE):
                rows = slice(tile * TILE, (tile + 1) * TILE)
                total = mb_ref[n, rows, :]
                across = bt_ref[n, rows, :]
                for g in range(GROUP):
                    place = g * nj + tile * TILE
                    if n == 0:
                        value = own_y[part][pl.ds(start + place, TILE), :]
                    else:
                        value = result[place : place + TILE, :]
                    total = total + scales[g] * value
                    sums[g] = sums[g] + across * value
                mb_ref[n, rows, :] = total
            for g in range(GROUP):
                ma_ref[n, pl.ds(first + g, 1), :] = jnp.sum(sums[g], axis=0, keepdims=True)

    sweep(ni // GROUP, contract, reduce, results)

    for n in range(2):
        rows_of[0, n * lanes : (n + 1) * lanes, :] = ma_ref[n].T
        rows_of[1, n * lanes : (n + 1) * lanes, :] = mb_ref[n].T
    for sz in range(nz):
        to_z = z ^ sz
        count = ny * ra + nx * rb + pa + pb
        put(
            sends[sz % 2].at[sz // 2 * count : (sz // 2 + 1) * count],
            [rows_of[0, pl.ds((((y ^ sy) * nz + to_z) * ra) ^ own, ra), :] for sy in range(ny)]
            + [rows_of[1, pl.ds((((x ^ sx) * nz + to_z) * rb) ^ own, rb), :] for sx in range(nx)]
            + [ca_ref[y * nz + to_z], cb_ref[x * nz + to_z]],
        )


def third_loop(turned, columns, weights_ref, result_refs, total_ref):
    total_ref[...] = jnp.zeros_like(total_ref)
    nk, lanes = total_ref.shape
    counts = [ref.shape[0] for ref in turned]

    def contract(turn, n, result):
        array, start, _ = spread(counts, turn, n)
        result[...] = product(flat(turned[array][pl.ds(start, GROUP)]), weights_ref[...])

    def reduce(turn, n, result):
        first = spread(counts, turn, n)[2]
        scales = [jnp.broadcast_to(columns[pl.ds(first + g, 1), :], (TILE, lanes)) for g in range(GROUP)]
        for tile in range(nk // TILE):
            rows = slice(tile * TILE, (tile + 1) * TILE)
            total = total_ref[rows, :]
            for g in range(GROUP):
                place = g * nk + tile * TILE
                total = total + scales[g] * result[place : place + TILE, :]
            total_ref[rows, :] = total

    sweep(sum(counts) // GROUP, contract, reduce, result_refs)


def partner_kernel(sizes, *refs):
    nx, ny, nz, ra, rb, rc = sizes
    (turned, (a_ref, at_ref, b_ref), sends), refs = take(refs, 3, 3, nx // 2)
    (kept_b, tb_ref, tc_ref, bb_ref, mc_ref, ba_ref, bc_ref), results, rows_of = refs[:7], refs[7:-1], refs[-1]
    x, y, z = here()
    lanes = mc_ref.shape[1]
    other = (1 - own_half(x, nx)) * lanes
    bb_ref[...] = weights(b_ref[pl.ds(other, lanes), :].T)
    gram = pair_grams(a_ref[...])
    tb_ref[...] = packed(gram, rb)
    tc_ref[...] = packed(gram, rc)
    gram = pair_grams(b_ref[...])
    ba_ref[...] = packed(gram, ra)
    bc_ref[...] = packed(gram, rc)
    third_loop(turned, at_ref.at[1], bb_ref, results, mc_ref)
    rows_of[...] = mc_ref[...].T
    for sx in range(nx // 2):
        to_x = x ^ (sx + nx // 2)
        put(
            sends[sx],
            [rows_of[pl.ds((to_x * ny + (y ^ sy)) * rc - other, rc), :] for sy in range(ny)]
            + [tb_ref[to_x * nz + z], tc_ref[to_x * ny + y]],
        )
    grams = []
    for sy in range(ny):
        grams += [ba_ref[(y ^ sy) * nz + z], bc_ref[x * ny + (y ^ sy)]]
    put(kept_b, grams)


def own_third_kernel(sizes, *refs):
    nx, ny, nz, ra, rb, rc = sizes
    (turned, (at_ref, b_ref, tb_ref, tc_ref), sends), refs = take(refs, 3, 4, nx // 2)
    (bb_ref, mc_ref), results, rows_of = refs[:2], refs[2:-1], refs[-1]
    x, y, z = here()
    lanes = mc_ref.shape[1]
    own = own_half(x, nx) * lanes
    bb_ref[...] = weights(b_ref[pl.ds(own, lanes), :].T)
    third_loop(turned, at_ref.at[0], bb_ref, results, mc_ref)
    rows_of[...] = mc_ref[...].T
    for sx in range(nx // 2):
        to_x = x ^ sx
        put(
            sends[sx],
            [rows_of[pl.ds((to_x * ny + (y ^ sy)) * rc - own, rc), :] for sy in range(ny)]
            + [tb_ref[to_x * nz + z], tc_ref[to_x * ny + y]],
        )


def core_kernel(sizes, own, other, *outs):
    count = outs[0].shape[0]
    for part, out in enumerate(outs):
        rows = slice(part * count, (part + 1) * count)
        out[...] = own[rows, :] + other[rows, :]


def middle_kernel(sizes, *refs):
    nx, ny, nz, ra, rb, rc = sizes
    (from_z, from_x, (grams_b,), for_y, for_x), (kept,) = take(refs, nz // 2, nx, 1, ny, nx)
    pa, pb, pc = packed_rows(ra), packed_rows(rb), packed_rows(rc)
    sum_z, sum_x = total_of(from_z), total_of(from_x)
    for sy in range(ny):
        put(
            for_y[sy],
            [
                sum_z[sy * ra : (sy + 1) * ra],
                sum_x[sy * rc : (sy + 1) * rc],
                grams_b[sy * (pa + pc) : (sy + 1) * (pa + pc), :],
            ],
        )
    for sx in range(nx):
        for_x[sx][...] = sum_z[ny * ra + sx * rb : ny * ra + (sx + 1) * rb]
    put(kept, [sum_z[ny * ra + nx * rb :], sum_x[ny * rc :]])


def scaled(one, other, rows, factor_ref, first_row):
    hessian = unpacked(one * other, rows)
    lane = lax.broadcasted_iota(jnp.int32, hessian.shape, 1)
    hessian = jnp.where(lane // R == lax.rem(first_row // R, 2), hessian, 0.0)
    pair = pl.multiple_of(first_row // PAIR * PAIR, PAIR)
    return accurate(hessian, factor_ref[pl.ds(pair, PAIR), :])


def grad_b_kernel(sizes, *refs):
    nx, ny, nz, ra, rb, rc = sizes
    (from_x, (kept, b_ref, grad_b)), _ = take(refs, nx, 3)
    pa, pb = packed_rows(ra), packed_rows(rb)
    x, y, z = here()
    gram_cb, gram_ab = kept[pa : pa + pb, :], kept[pa + pb : pa + 2 * pb, :]
    grad_b[...] = scaled(gram_ab, gram_cb, rb, b_ref, (x * nz + z) * rb) - total_of(from_x)


def last_kernel(sizes, *refs):
    nx, ny, nz, ra, rb, rc = sizes
    (from_y, (kept, a_ref, c_ref, grad_a, grad_c)), _ = take(refs, ny, 5)
    pa, pb = packed_rows(ra), packed_rows(rb)
    x, y, z = here()
    sum_y = total_of(from_y)
    m_a, m_c = sum_y[:ra], sum_y[ra : ra + rc]
    gram_ba, gram_bc = sum_y[ra + rc : ra + rc + pa], sum_y[ra + rc + pa :]
    gram_ca, gram_ac = kept[:pa, :], kept[pa + 2 * pb :, :]
    grad_a[...] = scaled(gram_ba, gram_ca, ra, a_ref, (y * nz + z) * ra) - m_a
    grad_c[...] = scaled(gram_ac, gram_bc, rc, c_ref, (x * ny + y) * rc) - m_c


def swap(value, axis, distance):
    return lax.ppermute(value, axis, [(i, i ^ distance) for i in range(lax.axis_size(axis))])


def partners(values, axis, stride=1):
    count = lax.axis_size(axis) // stride
    if not isinstance(values, (list, tuple)):
        values = [values] * count
    return [values[0]] + [swap(values[s], axis, s * stride) for s in range(1, count)]


def swapped(value):
    return swap(value, "gz", 1)


def body(tensor, factor_a, factor_b, factor_c):
    nx, ny, nz = (lax.axis_size(name) for name in ("gx", "gy", "gz"))
    ra, rb, rc = factor_a.shape[0], factor_b.shape[0], factor_c.shape[0]
    pa, pb, pc = packed_rows(ra), packed_rows(rb), packed_rows(rc)
    lanes = factor_a.shape[1]
    total = ra * ny * nz
    sizes = (nx, ny, nz, ra, rb, rc)
    message = ny * ra + nx * rb + pa + pb
    f32, bf16 = jnp.float32, jnp.bfloat16
    vmem = pl.BlockSpec(memory_space=pltpu.VMEM)
    tensor = pltpu.with_memory_space_constraint(tensor, pltpu.VMEM)
    flops = 2 * 3 * tensor.size * total

    def rows(count):
        return jax.ShapeDtypeStruct((count, lanes), f32)

    def call(kernel, outs, args, scratch=(), limit=4, cost=None, space=pltpu.VMEM):
        return pl.pallas_call(
            lambda *refs: kernel(sizes, *refs),
            out_shape=outs,
            in_specs=[pl.BlockSpec(memory_space=space)] * len(args),
            out_specs=[vmem] * len(outs),
            scratch_shapes=scratch,
            compiler_params=pltpu.CompilerParams(vmem_limit_bytes=limit * MIB),
            cost_estimate=cost,
            name=kernel.__name__,
        )(*args)

    work = pl.CostEstimate(flops=flops, bytes_accessed=4 * tensor.size, transcendentals=0)

    ni, nj, nk = tensor.shape
    half = total // 2
    results = [pltpu.VMEM((GROUP * nj, half), f32)] * BUFFERS
    weight = pltpu.VMEM((2 * lanes, 2 * half), bf16)
    halves = pltpu.VMEM((2, lanes, half), f32)
    later = ni // 2

    def own_part(count):
        return pltpu.VMEM((count * nj, half), f32)

    def slices(count):
        return pltpu.VMEM((count, nk, 2 * nj), bf16)

    def gram_blocks(count):
        return pltpu.VMEM((total // count, packed_rows(count), PAIR), f32)

    def array(ref):
        return jax.ShapeDtypeStruct(ref.shape, ref.dtype)

    own_ac, own_b = call(
        own_kernel,
        [rows(ra + rc), rows(rb)],
        [pltpu.with_memory_space_constraint(value, pltpu.HBM) for value in (factor_a, factor_b, factor_c)],
        [pltpu.SemaphoreType.DMA((3,))],
        cost=work,
        space=pltpu.HBM,
    )
    ac = partners(own_ac, "gy")
    b = partners(own_b, "gx")
    pairs, turned_0, rows_b = call(
        tensor_kernel, [slices(ni), slices(ni // 2), rows(nx * rb)], [*b, tensor], (), 8, work
    )
    for_z, for_x = call(pack_kernel, [rows(ny * ra + nx * rb), rows(ny * rc)], [*ac, rows_b])
    from_x = partners(for_x, "gx")
    by_x = partners(for_z, "gz", 2)
    own_y_0, turned_1, own_c, weights_c = call(
        early_kernel,
        [own_part(ni - later), slices((ni - later) // 2), rows(half), array(weight)],
        [*from_x[: nx // 2], pairs],
        (),
        8,
        work,
    )
    (stack,) = call(stack_kernel, [rows(nz // 2 * (ny * ra + nx * rb))], [*by_x, own_c])
    from_z = [stack, swapped(stack)]
    own_y_1, turned_2 = call(later_kernel, [own_part(later), slices(later // 2)], [pairs, weights_c], (), 8, work)
    turned = [turned_0, turned_1, turned_2]
    own_core, other_core, block_a, columns_a, block_b, block_c = call(
        first_kernel,
        [rows(nz // 2 * message)] * 2 + [rows(total), array(halves), rows(total), rows(total)],
        [*from_z, *from_x[nx // 2 :], own_y_0, own_y_1, own_c, pairs],
        [
            halves, weight, halves, halves, gram_blocks(ra), gram_blocks(rb),
            *results, pltpu.VMEM((2, total, lanes), f32),
        ],
        12,
        work,
    )
    other_core = swapped(other_core)
    outs = call(
        partner_kernel,
        [rows(ny * rc + pb + pc)] * (nx // 2)
        + [rows(ny * (pa + pc)), array(gram_blocks(rb)), array(gram_blocks(rc))],
        [*turned, block_a, columns_a, block_b],
        [
            weight, pltpu.VMEM((nk, half), f32), gram_blocks(ra), gram_blocks(rc),
            *results, pltpu.VMEM((half, lanes), f32),
        ],
        8,
        work,
    )
    sums_x, (grams_b, grams_ab, grams_ac) = outs[: nx // 2], outs[nx // 2 :]
    sums_x = [swap(value, "gx", s + nx // 2) for s, value in enumerate(sums_x)]
    sums_z = call(core_kernel, [rows(message)] * (nz // 2), [own_core, other_core])
    sums_z = partners(sums_z, "gz", 2)
    own_x = call(
        own_third_kernel,
        [rows(ny * rc + pb + pc)] * (nx // 2),
        [*turned, columns_a, block_b, grams_ab, grams_ac],
        [weight, pltpu.VMEM((nk, half), f32), *results, pltpu.VMEM((half, lanes), f32)],
        8,
        work,
    )
    sums_x = [swap(value, "gx", s) if s else value for s, value in enumerate(own_x)] + sums_x
    outs = call(
        middle_kernel,
        [rows(ra + rc + pa + pc)] * ny + [rows(rb)] * nx + [rows(pa + pb + pb + pc)],
        [*sums_z, *sums_x, grams_b],
    )
    sums_y, sums_x, kept = outs[:ny], outs[ny : ny + nx], outs[ny + nx]
    sums_y = partners(sums_y, "gy")
    sums_x = partners(sums_x, "gx")
    (grad_b,) = call(grad_b_kernel, [rows(rb)], [*sums_x, kept, block_b], cost=work)
    grad_a, grad_c = call(last_kernel, [rows(ra), rows(rc)], [*sums_y[::-1], kept, block_a, block_c])
    return grad_a, grad_b, grad_c


def solution(mesh):
    in_specs = (
        P("gx", "gy", "gz"),
        P(("gy", "gz"), "gx"),
        P(("gx", "gz"), "gy"),
        P(("gx", "gy"), "gz"),
    )
    out_specs = (P(("gy", "gz"), "gx"), P(("gx", "gz"), "gy"), P(("gx", "gy"), "gz"))
    return jax.shard_map(body, mesh=mesh, in_specs=in_specs, out_specs=out_specs, check_vma=False)
```

```python
import jax
import jax.numpy as jnp
from jax import lax
from jax.experimental import pallas as pl
from jax.experimental.pallas import tpu as pltpu
from jax.sharding import PartitionSpec as P

R = 64
PAIR = 2 * R
GROUP = 8
UNROLL = 16
BUFFERS = 8
TILE = 8
TURNS = 64
MIB = 1024 * 1024


def split(value):
    high = value.astype(jnp.bfloat16)
    low = (value - high.astype(jnp.float32)).astype(jnp.bfloat16)
    return high, low


def pair_grams(rows):
    row = lax.broadcasted_iota(jnp.int32, (PAIR, PAIR), 0) // R
    col = lax.broadcasted_iota(jnp.int32, (PAIR, PAIR), 1) // R
    blocks = []
    for pair in range(rows.shape[0] // PAIR):
        part = rows[pair * PAIR : (pair + 1) * PAIR, :]
        high, low = split(part)
        gram = lax.dot_general(
            jnp.concatenate([high, low, high], axis=1),
            jnp.concatenate([high, high, low], axis=1),
            (((1,), (1,)), ((), ())),
            preferred_element_type=jnp.float32,
        )
        blocks.append(folded(jnp.where(row == col, gram, 0.0)))
    return jnp.concatenate(blocks, axis=0)


def folded(value):
    half = value.shape[1] // 2
    return value + jnp.concatenate([value[:, half:], value[:, :half]], axis=1)


def packs(rows):
    return rows % 16 == 0


def packed_rows(rows):
    return rows // 2 if packs(rows) else rows


def packed(gram, rows):
    blocks = gram.reshape(-1, rows, gram.shape[1])
    if not packs(rows):
        return blocks
    half = rows // 2
    lane = lax.broadcasted_iota(jnp.int32, (blocks.shape[0], half, gram.shape[1]), 2)
    return jnp.where(lane < R, blocks[:, :half], blocks[:, half:])


def unpacked(block, rows):
    if not packs(rows):
        return block
    lane = lax.broadcasted_iota(jnp.int32, block.shape, 1)
    return folded(jnp.concatenate([jnp.where(lane < R, block, 0.0), jnp.where(lane < R, 0.0, block)], axis=0))


def here():
    return lax.axis_index("gx"), lax.axis_index("gy"), lax.axis_index("gz")


def take(refs, *counts):
    groups, first = [], 0
    for count in counts:
        groups.append(refs[first : first + count])
        first += count
    return groups, refs[first:]


def put(ref, values):
    first = 0
    for value in values:
        ref[first : first + value.shape[0], :] = value
        first += value.shape[0]


def total_of(refs):
    total = refs[0][...]
    for ref in refs[1:]:
        total = total + ref[...]
    return total


def token_kernel(sizes, token):
    token[...] = jnp.zeros_like(token)


def own_kernel(sizes, a_ref, c_ref, _, ac_ref):
    put(ac_ref, [a_ref[...], c_ref[...]])


def pack_kernel(sizes, *refs):
    nx, ny, nz, ra, rb, rc = sizes
    (ac, (b, for_z, for_x)), _ = take(refs, ny, 3)
    put(for_z, [ref[:ra, :] for ref in ac] + [b[...]])
    put(for_x, [ref[ra:, :] for ref in ac])


def sweep(blocks, contract, reduce, results):
    @pl.loop(0, blocks // UNROLL)
    def _(turn):
        for n in range(UNROLL + 1):
            if n < UNROLL:
                contract(turn, n, results[n % BUFFERS])
            if n:
                reduce(turn, n - 1, results[(n - 1) % BUFFERS])


def spread(counts, turn, n):
    turns = sum(counts) // (GROUP * UNROLL)
    first = 0
    for array, count in enumerate(counts):
        share = count // (GROUP * turns)
        if n < share:
            start = (turn * share + n) * GROUP
            return array, pl.multiple_of(start, GROUP), pl.multiple_of(first + start, GROUP)
        n -= share
        first += count


def weights(columns):
    both = jnp.concatenate(split(columns), axis=1)
    return jnp.concatenate([both, both], axis=0)


def product(pair, weights):
    value = jnp.dot(pair, weights, preferred_element_type=jnp.float32)
    half = value.shape[1] // 2
    return value[:, :half] + value[:, half:]


def flat(block):
    return block.reshape(block.shape[0] * block.shape[1], block.shape[2])


def transpose(pairs, first, turned, start, count):
    for n in range(count):
        turned[start + n] = transposed(pairs[first + n])


def transposed(pair):
    half = pair.shape[1] // 2
    return jnp.concatenate([pair[:, :half].T, pair[:, half:].T], axis=1)


def tensor_kernel(sizes, *refs):
    (b, (tensor, pairs, turned, rows_b)), _ = take(refs, sizes[0], 4)
    put(rows_b, [ref[...] for ref in b])

    @pl.loop(0, tensor.shape[0] // (2 * TURNS))
    def _(turn):
        for n in range(2 * TURNS):
            place = turn * 2 * TURNS + n
            pair = jnp.concatenate(split(tensor[place]), axis=1)
            pairs[place] = pair
        for n in range(TURNS):
            transpose(pairs, turn * TURNS + n, turned, turn * TURNS + n, 1)


def own_half(x, nx):
    return x // (nx // 2)


def early_columns(sizes, packs_x, c_ref):
    nx, ny, nz, ra, rb, rc = sizes
    x, y, z = here()
    part = lax.rem(x, nx // 2)
    for sx in range(nx // 2):
        for sy in range(ny):
            place = ((part ^ sx) * ny + (y ^ sy)) * rc
            c_ref[pl.ds(place, rc), :] = packs_x[sx][sy * rc : (sy + 1) * rc, :]


def early_loop(first, count, pairs, weights_ref, own_y, turned):
    nj = pairs.shape[1]
    turns = GROUP // 2
    start = pairs.shape[0] // 2 + first // 2
    for block in range(count // GROUP):
        own_y[pl.ds(block * GROUP * nj, GROUP * nj), :] = product(
            flat(pairs[pl.ds(first + block * GROUP, GROUP)]), weights_ref[...]
        )
        transpose(pairs, start + block * turns, turned, block * turns, turns)


def early_kernel(sizes, *refs):
    (packs_x, (pairs, own_y, turned, c_ref, cc_ref)), _ = take(refs, sizes[0] // 2, 5)
    early_columns(sizes, packs_x, c_ref)
    cc_ref[...] = weights(c_ref[...].T)
    early_loop(0, own_y.shape[0] // pairs.shape[1], pairs, cc_ref, own_y, turned)


def later_kernel(sizes, pairs, cc_ref, own_y, turned):
    count = own_y.shape[0] // pairs.shape[1]
    early_loop(pairs.shape[0] - count, count, pairs, cc_ref, own_y, turned)


def stack_kernel(sizes, *refs):
    *values, _, target = refs
    put(target, [value[...] for value in values])


def first_kernel(sizes, *refs):
    nx, ny, nz, ra, rb, rc = sizes
    (packs_z, packs_x, own_y, (own_c, pairs), sends), refs = take(refs, 2, nx // 2, 2, 2, 2)
    a_ref, at_ref, b_ref, c_ref, bt_ref, cc_ref, ma_ref, mb_ref = refs[:8]
    (ca_ref, cb_ref), results, (rows_of,) = refs[8:10], refs[10:-1], refs[-1:]
    pa, pb = packed_rows(ra), packed_rows(rb)
    x, y, z = here()
    ni, nj = pairs.shape[0], pairs.shape[1]
    lanes = c_ref.shape[0] // 2
    half = own_half(x, nx)
    own, other = half * lanes, (1 - half) * lanes

    for sz in range(nz):
        start = sz // 2 * (ny * ra + nx * rb)
        for sy in range(ny):
            a_ref[pl.ds(((y ^ sy) * nz + (z ^ sz)) * ra, ra), :] = packs_z[sz % 2][start : start + ra, :]
            start += ra
        for sx in range(nx):
            b_ref[pl.ds(((x ^ sx) * nz + (z ^ sz)) * rb, rb), :] = packs_z[sz % 2][start : start + rb, :]
            start += rb
    c_ref[pl.ds(own, lanes), :] = own_c[...]
    for sx in range(nx // 2):
        for sy in range(ny):
            place = ((x ^ (sx + nx // 2)) * ny + (y ^ sy)) * rc
            c_ref[pl.ds(place, rc), :] = packs_x[sx][sy * rc : (sy + 1) * rc, :]
    for n, first in enumerate((own, other)):
        at_ref[n] = a_ref[pl.ds(first, lanes), :].T
        bt_ref[n] = b_ref[pl.ds(first, lanes), :].T
    cc_ref[...] = weights(c_ref[pl.ds(other, lanes), :].T)
    gram = pair_grams(c_ref[...])
    ca_ref[...] = packed(gram, ra)
    cb_ref[...] = packed(gram, rb)
    mb_ref[...] = jnp.zeros_like(mb_ref)

    counts = [ref.shape[0] // nj for ref in own_y]

    def contract(turn, n, result):
        slices = spread(counts, turn, n)[2]
        result[...] = product(flat(pairs[pl.ds(slices, GROUP)]), cc_ref[...])

    def reduce(turn, n, result):
        part, start, first = spread(counts, turn, n)
        start = pl.multiple_of(start * nj, GROUP * nj)
        for n in range(2):
            scales = [jnp.broadcast_to(at_ref[n, pl.ds(first + g, 1), :], (TILE, lanes)) for g in range(GROUP)]
            sums = [jnp.zeros((TILE, lanes), jnp.float32)] * GROUP
            for tile in range(nj // TILE):
                rows = slice(tile * TILE, (tile + 1) * TILE)
                total = mb_ref[n, rows, :]
                across = bt_ref[n, rows, :]
                for g in range(GROUP):
                    place = g * nj + tile * TILE
                    if n == 0:
                        value = own_y[part][pl.ds(start + place, TILE), :]
                    else:
                        value = result[place : place + TILE, :]
                    total = total + scales[g] * value
                    sums[g] = sums[g] + across * value
                mb_ref[n, rows, :] = total
            for g in range(GROUP):
                ma_ref[n, pl.ds(first + g, 1), :] = jnp.sum(sums[g], axis=0, keepdims=True)

    sweep(ni // GROUP, contract, reduce, results)

    for n in range(2):
        rows_of[0, n * lanes : (n + 1) * lanes, :] = ma_ref[n].T
        rows_of[1, n * lanes : (n + 1) * lanes, :] = mb_ref[n].T
    for sz in range(nz):
        to_z = z ^ sz
        count = ny * ra + nx * rb + pa + pb
        put(
            sends[sz % 2].at[sz // 2 * count : (sz // 2 + 1) * count],
            [rows_of[0, pl.ds((((y ^ sy) * nz + to_z) * ra) ^ own, ra), :] for sy in range(ny)]
            + [rows_of[1, pl.ds((((x ^ sx) * nz + to_z) * rb) ^ own, rb), :] for sx in range(nx)]
            + [ca_ref[y * nz + to_z], cb_ref[x * nz + to_z]],
        )


def third_loop(turned, columns, weights_ref, result_refs, total_ref):
    total_ref[...] = jnp.zeros_like(total_ref)
    nk, lanes = total_ref.shape
    counts = [ref.shape[0] for ref in turned]

    def contract(turn, n, result):
        array, start, _ = spread(counts, turn, n)
        result[...] = product(flat(turned[array][pl.ds(start, GROUP)]), weights_ref[...])

    def reduce(turn, n, result):
        first = spread(counts, turn, n)[2]
        scales = [jnp.broadcast_to(columns[pl.ds(first + g, 1), :], (TILE, lanes)) for g in range(GROUP)]
        for tile in range(nk // TILE):
            rows = slice(tile * TILE, (tile + 1) * TILE)
            total = total_ref[rows, :]
            for g in range(GROUP):
                place = g * nk + tile * TILE
                total = total + scales[g] * result[place : place + TILE, :]
            total_ref[rows, :] = total

    sweep(sum(counts) // GROUP, contract, reduce, result_refs)


def partner_kernel(sizes, *refs):
    nx, ny, nz, ra, rb, rc = sizes
    (turned, (a_ref, at_ref, b_ref), sends), refs = take(refs, 3, 3, nx // 2)
    (kept_b, tb_ref, tc_ref, bb_ref, mc_ref, ba_ref, bc_ref), results, rows_of = refs[:7], refs[7:-1], refs[-1]
    x, y, z = here()
    lanes = mc_ref.shape[1]
    other = (1 - own_half(x, nx)) * lanes
    bb_ref[...] = weights(b_ref[pl.ds(other, lanes), :].T)
    gram = pair_grams(a_ref[...])
    tb_ref[...] = packed(gram, rb)
    tc_ref[...] = packed(gram, rc)
    gram = pair_grams(b_ref[...])
    ba_ref[...] = packed(gram, ra)
    bc_ref[...] = packed(gram, rc)
    third_loop(turned, at_ref.at[1], bb_ref, results, mc_ref)
    rows_of[...] = mc_ref[...].T
    for sx in range(nx // 2):
        to_x = x ^ (sx + nx // 2)
        put(
            sends[sx],
            [rows_of[pl.ds((to_x * ny + (y ^ sy)) * rc - other, rc), :] for sy in range(ny)]
            + [tb_ref[to_x * nz + z], tc_ref[to_x * ny + y]],
        )
    grams = []
    for sy in range(ny):
        grams += [ba_ref[(y ^ sy) * nz + z], bc_ref[x * ny + (y ^ sy)]]
    put(kept_b, grams)


def own_third_kernel(sizes, *refs):
    nx, ny, nz, ra, rb, rc = sizes
    (turned, (at_ref, b_ref, tb_ref, tc_ref), sends), refs = take(refs, 3, 4, nx // 2)
    (bb_ref, mc_ref), results, rows_of = refs[:2], refs[2:-1], refs[-1]
    x, y, z = here()
    lanes = mc_ref.shape[1]
    own = own_half(x, nx) * lanes
    bb_ref[...] = weights(b_ref[pl.ds(own, lanes), :].T)
    third_loop(turned, at_ref.at[0], bb_ref, results, mc_ref)
    rows_of[...] = mc_ref[...].T
    for sx in range(nx // 2):
        to_x = x ^ sx
        put(
            sends[sx],
            [rows_of[pl.ds((to_x * ny + (y ^ sy)) * rc - own, rc), :] for sy in range(ny)]
            + [tb_ref[to_x * nz + z], tc_ref[to_x * ny + y]],
        )


def core_kernel(sizes, own, other, *outs):
    count = outs[0].shape[0]
    for part, out in enumerate(outs):
        rows = slice(part * count, (part + 1) * count)
        out[...] = own[rows, :] + other[rows, :]


def middle_kernel(sizes, *refs):
    nx, ny, nz, ra, rb, rc = sizes
    (from_z, from_x, (grams_b,), for_y, for_x), (kept,) = take(refs, nz // 2, nx, 1, ny, nx)
    pa, pb, pc = packed_rows(ra), packed_rows(rb), packed_rows(rc)
    sum_z, sum_x = total_of(from_z), total_of(from_x)
    for sy in range(ny):
        put(
            for_y[sy],
            [
                sum_z[sy * ra : (sy + 1) * ra],
                sum_x[sy * rc : (sy + 1) * rc],
                grams_b[sy * (pa + pc) : (sy + 1) * (pa + pc), :],
            ],
        )
    for sx in range(nx):
        for_x[sx][...] = sum_z[ny * ra + sx * rb : ny * ra + (sx + 1) * rb]
    put(kept, [sum_z[ny * ra + nx * rb :], sum_x[ny * rc :]])


def scaled(one, other, rows, pair_weights, first_row):
    hessian = unpacked(one * other, rows)
    lane = lax.broadcasted_iota(jnp.int32, hessian.shape, 1)
    hessian = jnp.where(lane // R == lax.rem(first_row // R, 2), hessian, 0.0)
    return product(jnp.concatenate(split(hessian), axis=1), pair_weights)


def pair_weights(factor_ref, first_row):
    pair = pl.multiple_of(first_row // PAIR * PAIR, PAIR)
    return weights(factor_ref[pl.ds(pair, PAIR), :])


def grad_b_kernel(sizes, *refs):
    nx, ny, nz, ra, rb, rc = sizes
    (from_x, (kept, a_ref, b_ref, c_ref, grad_b, weights_a, weights_c)), _ = take(refs, nx, 7)
    pa, pb = packed_rows(ra), packed_rows(rb)
    x, y, z = here()
    gram_cb, gram_ab = kept[pa : pa + pb, :], kept[pa + pb : pa + 2 * pb, :]
    first = (x * nz + z) * rb
    grad_b[...] = scaled(gram_ab, gram_cb, rb, pair_weights(b_ref, first), first) - total_of(from_x)
    weights_a[...] = pair_weights(a_ref, (y * nz + z) * ra)
    weights_c[...] = pair_weights(c_ref, (x * ny + y) * rc)


def last_kernel(sizes, *refs):
    nx, ny, nz, ra, rb, rc = sizes
    (from_y, (kept, weights_a, weights_c, grad_a, grad_c)), _ = take(refs, ny, 5)
    pa, pb = packed_rows(ra), packed_rows(rb)
    x, y, z = here()
    sum_y = total_of(from_y)
    m_a, m_c = sum_y[:ra], sum_y[ra : ra + rc]
    gram_ba, gram_bc = sum_y[ra + rc : ra + rc + pa], sum_y[ra + rc + pa :]
    gram_ca, gram_ac = kept[:pa, :], kept[pa + 2 * pb :, :]
    grad_a[...] = scaled(gram_ba, gram_ca, ra, weights_a[...], (y * nz + z) * ra) - m_a
    grad_c[...] = scaled(gram_ac, gram_bc, rc, weights_c[...], (x * ny + y) * rc) - m_c


def swap(value, axis, distance):
    return lax.ppermute(value, axis, [(i, i ^ distance) for i in range(lax.axis_size(axis))])


def partners(values, axis, stride=1):
    count = lax.axis_size(axis) // stride
    if not isinstance(values, (list, tuple)):
        values = [values] * count
    return [values[0]] + [swap(values[s], axis, s * stride) for s in range(1, count)]


def swapped(value):
    return swap(value, "gz", 1)


def body(tensor, factor_a, factor_b, factor_c):
    nx, ny, nz = (lax.axis_size(name) for name in ("gx", "gy", "gz"))
    ra, rb, rc = factor_a.shape[0], factor_b.shape[0], factor_c.shape[0]
    pa, pb, pc = packed_rows(ra), packed_rows(rb), packed_rows(rc)
    lanes = factor_a.shape[1]
    total = ra * ny * nz
    sizes = (nx, ny, nz, ra, rb, rc)
    message = ny * ra + nx * rb + pa + pb
    f32, bf16 = jnp.float32, jnp.bfloat16
    vmem = pl.BlockSpec(memory_space=pltpu.VMEM)
    tensor = pltpu.with_memory_space_constraint(tensor, pltpu.VMEM)
    flops = 2 * 3 * tensor.size * total

    def rows(count):
        return jax.ShapeDtypeStruct((count, lanes), f32)

    def call(kernel, outs, args, scratch=(), limit=4, cost=None, space=pltpu.VMEM):
        return pl.pallas_call(
            lambda *refs: kernel(sizes, *refs),
            out_shape=outs,
            in_specs=[pl.BlockSpec(memory_space=space)] * len(args),
            out_specs=[vmem] * len(outs),
            scratch_shapes=scratch,
            compiler_params=pltpu.CompilerParams(vmem_limit_bytes=limit * MIB),
            cost_estimate=cost,
            name=kernel.__name__,
        )(*args)

    work = pl.CostEstimate(flops=flops, bytes_accessed=4 * tensor.size, transcendentals=0)

    ni, nj, nk = tensor.shape
    half = total // 2
    results = [pltpu.VMEM((GROUP * nj, half), f32)] * BUFFERS
    weight = pltpu.VMEM((2 * lanes, 2 * half), bf16)
    halves = pltpu.VMEM((2, lanes, half), f32)
    later = ni // 2

    def own_part(count):
        return pltpu.VMEM((count * nj, half), f32)

    def slices(count):
        return pltpu.VMEM((count, nk, 2 * nj), bf16)

    def gram_blocks(count):
        return pltpu.VMEM((total // count, packed_rows(count), PAIR), f32)

    def array(ref):
        return jax.ShapeDtypeStruct(ref.shape, ref.dtype)

    (token,) = call(token_kernel, [rows(TILE)], [], cost=work)
    (own_ac,) = call(
        own_kernel,
        [rows(ra + rc)],
        [*(pltpu.with_memory_space_constraint(value, pltpu.VMEM) for value in (factor_a, factor_c)), token],
        cost=work,
    )
    ac = partners(own_ac, "gy")
    b = partners(factor_b, "gx")
    pairs, turned_0, rows_b = call(
        tensor_kernel, [slices(ni), slices(ni // 2), rows(nx * rb)], [*b, tensor], (), 8, work
    )
    for_z, for_x = call(pack_kernel, [rows(ny * ra + nx * rb), rows(ny * rc)], [*ac, rows_b])
    from_x = partners(for_x, "gx")
    by_x = partners(for_z, "gz", 2)
    own_y_0, turned_1, own_c, weights_c = call(
        early_kernel,
        [own_part(ni - later), slices((ni - later) // 2), rows(half), array(weight)],
        [*from_x[: nx // 2], pairs],
        (),
        8,
        work,
    )
    (stack,) = call(stack_kernel, [rows(nz // 2 * (ny * ra + nx * rb))], [*by_x, own_c])
    from_z = [stack, swapped(stack)]
    own_y_1, turned_2 = call(later_kernel, [own_part(later), slices(later // 2)], [pairs, weights_c], (), 8, work)
    turned = [turned_0, turned_1, turned_2]
    own_core, other_core, block_a, columns_a, block_b, block_c = call(
        first_kernel,
        [rows(nz // 2 * message)] * 2 + [rows(total), array(halves), rows(total), rows(total)],
        [*from_z, *from_x[nx // 2 :], own_y_0, own_y_1, own_c, pairs],
        [
            halves, weight, halves, halves, gram_blocks(ra), gram_blocks(rb),
            *results, pltpu.VMEM((2, total, lanes), f32),
        ],
        12,
        work,
    )
    other_core = swapped(other_core)
    outs = call(
        partner_kernel,
        [rows(ny * rc + pb + pc)] * (nx // 2)
        + [rows(ny * (pa + pc)), array(gram_blocks(rb)), array(gram_blocks(rc))],
        [*turned, block_a, columns_a, block_b],
        [
            weight, pltpu.VMEM((nk, half), f32), gram_blocks(ra), gram_blocks(rc),
            *results, pltpu.VMEM((half, lanes), f32),
        ],
        8,
        work,
    )
    sums_x, (grams_b, grams_ab, grams_ac) = outs[: nx // 2], outs[nx // 2 :]
    sums_x = [swap(value, "gx", s + nx // 2) for s, value in enumerate(sums_x)]
    sums_z = call(core_kernel, [rows(message)] * (nz // 2), [own_core, other_core])
    sums_z = partners(sums_z, "gz", 2)
    own_x = call(
        own_third_kernel,
        [rows(ny * rc + pb + pc)] * (nx // 2),
        [*turned, columns_a, block_b, grams_ab, grams_ac],
        [weight, pltpu.VMEM((nk, half), f32), *results, pltpu.VMEM((half, lanes), f32)],
        8,
        work,
    )
    sums_x = [swap(value, "gx", s) if s else value for s, value in enumerate(own_x)] + sums_x
    outs = call(
        middle_kernel,
        [rows(ra + rc + pa + pc)] * ny + [rows(rb)] * nx + [rows(pa + pb + pb + pc)],
        [*sums_z, *sums_x, grams_b],
    )
    sums_y, sums_x, kept = outs[:ny], outs[ny : ny + nx], outs[ny + nx]
    sums_y = partners(sums_y, "gy")
    sums_x = partners(sums_x, "gx")
    pair = pltpu.VMEM((2 * PAIR, 2 * lanes), bf16)
    grad_b, weights_a, weights_c = call(
        grad_b_kernel,
        [rows(rb), array(pair), array(pair)],
        [*sums_x, kept, block_a, block_b, block_c],
        cost=work,
    )
    grad_a, grad_c = call(last_kernel, [rows(ra), rows(rc)], [*sums_y[::-1], kept, weights_a, weights_c])
    return grad_a, grad_b, grad_c


def solution(mesh):
    in_specs = (
        P("gx", "gy", "gz"),
        P(("gy", "gz"), "gx"),
        P(("gx", "gz"), "gy"),
        P(("gx", "gy"), "gz"),
    )
    out_specs = (P(("gy", "gz"), "gx"), P(("gx", "gz"), "gy"), P(("gx", "gy"), "gz"))
    return jax.shard_map(body, mesh=mesh, in_specs=in_specs, out_specs=out_specs, check_vma=False)
```

```python
import jax
import jax.numpy as jnp
from jax import lax
from jax.experimental import pallas as pl
from jax.experimental.pallas import tpu as pltpu
from jax.sharding import PartitionSpec as P

R = 64
PAIR = 2 * R
GROUP = 4
UNROLL = 32
BUFFERS = 8
TILE = 8
TURNS = 64
MIB = 1024 * 1024


def split(value):
    high = value.astype(jnp.bfloat16)
    low = (value - high.astype(jnp.float32)).astype(jnp.bfloat16)
    return high, low


def pair_grams(rows):
    row = lax.broadcasted_iota(jnp.int32, (PAIR, PAIR), 0) // R
    col = lax.broadcasted_iota(jnp.int32, (PAIR, PAIR), 1) // R
    blocks = []
    for pair in range(rows.shape[0] // PAIR):
        part = rows[pair * PAIR : (pair + 1) * PAIR, :]
        high, low = split(part)
        gram = lax.dot_general(
            jnp.concatenate([high, low, high], axis=1),
            jnp.concatenate([high, high, low], axis=1),
            (((1,), (1,)), ((), ())),
            preferred_element_type=jnp.float32,
        )
        blocks.append(folded(jnp.where(row == col, gram, 0.0)))
    return jnp.concatenate(blocks, axis=0)


def folded(value):
    half = value.shape[1] // 2
    return value + jnp.concatenate([value[:, half:], value[:, :half]], axis=1)


def packs(rows):
    return rows % 16 == 0


def packed_rows(rows):
    return rows // 2 if packs(rows) else rows


def packed(gram, rows):
    blocks = gram.reshape(-1, rows, gram.shape[1])
    if not packs(rows):
        return blocks
    half = rows // 2
    lane = lax.broadcasted_iota(jnp.int32, (blocks.shape[0], half, gram.shape[1]), 2)
    return jnp.where(lane < R, blocks[:, :half], blocks[:, half:])


def unpacked(block, rows):
    if not packs(rows):
        return block
    lane = lax.broadcasted_iota(jnp.int32, block.shape, 1)
    return folded(jnp.concatenate([jnp.where(lane < R, block, 0.0), jnp.where(lane < R, 0.0, block)], axis=0))


def here():
    return lax.axis_index("gx"), lax.axis_index("gy"), lax.axis_index("gz")


def take(refs, *counts):
    groups, first = [], 0
    for count in counts:
        groups.append(refs[first : first + count])
        first += count
    return groups, refs[first:]


def put(ref, values):
    first = 0
    for value in values:
        ref[first : first + value.shape[0], :] = value
        first += value.shape[0]


def total_of(refs):
    total = refs[0][...]
    for ref in refs[1:]:
        total = total + ref[...]
    return total


def token_kernel(sizes, token):
    token[...] = jnp.zeros_like(token)


def own_kernel(sizes, a_ref, c_ref, _, ac_ref):
    put(ac_ref, [a_ref[...], c_ref[...]])


def pack_kernel(sizes, *refs):
    nx, ny, nz, ra, rb, rc = sizes
    (ac, (b, for_z, for_x)), _ = take(refs, ny, 3)
    put(for_z, [ref[:ra, :] for ref in ac] + [b[...]])
    put(for_x, [ref[ra:, :] for ref in ac])


def sweep(blocks, contract, reduce, results):
    @pl.loop(0, blocks // UNROLL)
    def _(turn):
        for n in range(UNROLL + 1):
            if n < UNROLL:
                contract(turn, n, results[n % BUFFERS])
            if n:
                reduce(turn, n - 1, results[(n - 1) % BUFFERS])


def spread(counts, turn, n):
    turns = sum(counts) // (GROUP * UNROLL)
    first = 0
    for array, count in enumerate(counts):
        share = count // (GROUP * turns)
        if n < share:
            start = (turn * share + n) * GROUP
            return array, pl.multiple_of(start, GROUP), pl.multiple_of(first + start, GROUP)
        n -= share
        first += count


def weights(columns):
    both = jnp.concatenate(split(columns), axis=1)
    return jnp.concatenate([both, both], axis=0)


def product(pair, weights):
    value = jnp.dot(pair, weights, preferred_element_type=jnp.float32)
    half = value.shape[1] // 2
    return value[:, :half] + value[:, half:]


def flat(block):
    return block.reshape(block.shape[0] * block.shape[1], block.shape[2])


def transpose(pairs, first, turned, start, count):
    for n in range(count):
        turned[start + n] = transposed(pairs[first + n])


def transposed(pair):
    half = pair.shape[1] // 2
    return jnp.concatenate([pair[:, :half].T, pair[:, half:].T], axis=1)


def tensor_kernel(sizes, *refs):
    (b, (tensor, pairs, turned, rows_b)), _ = take(refs, sizes[0], 4)
    put(rows_b, [ref[...] for ref in b])

    @pl.loop(0, tensor.shape[0] // (2 * TURNS))
    def _(turn):
        for n in range(2 * TURNS):
            place = turn * 2 * TURNS + n
            pair = jnp.concatenate(split(tensor[place]), axis=1)
            pairs[place] = pair
        for n in range(TURNS):
            transpose(pairs, turn * TURNS + n, turned, turn * TURNS + n, 1)


def own_half(x, nx):
    return x // (nx // 2)


def early_columns(sizes, packs_x, c_ref):
    nx, ny, nz, ra, rb, rc = sizes
    x, y, z = here()
    part = lax.rem(x, nx // 2)
    for sx in range(nx // 2):
        for sy in range(ny):
            place = ((part ^ sx) * ny + (y ^ sy)) * rc
            c_ref[pl.ds(place, rc), :] = packs_x[sx][sy * rc : (sy + 1) * rc, :]


def early_loop(first, count, pairs, weights_ref, own_y, turned):
    nj = pairs.shape[1]
    turns = GROUP // 2
    start = pairs.shape[0] // 2 + first // 2
    for block in range(count // GROUP):
        own_y[pl.ds(block * GROUP * nj, GROUP * nj), :] = product(
            flat(pairs[pl.ds(first + block * GROUP, GROUP)]), weights_ref[...]
        )
        transpose(pairs, start + block * turns, turned, block * turns, turns)


def early_kernel(sizes, *refs):
    (packs_x, (pairs, own_y, turned, c_ref, cc_ref)), _ = take(refs, sizes[0] // 2, 5)
    early_columns(sizes, packs_x, c_ref)
    cc_ref[...] = weights(c_ref[...].T)
    early_loop(0, own_y.shape[0] // pairs.shape[1], pairs, cc_ref, own_y, turned)


def later_kernel(sizes, pairs, cc_ref, own_y, turned):
    count = own_y.shape[0] // pairs.shape[1]
    early_loop(pairs.shape[0] - count, count, pairs, cc_ref, own_y, turned)


def stack_kernel(sizes, *refs):
    *values, _, target = refs
    put(target, [value[...] for value in values])


def first_kernel(sizes, *refs):
    nx, ny, nz, ra, rb, rc = sizes
    (packs_z, packs_x, own_y, (own_c, pairs), sends), refs = take(refs, 2, nx // 2, 2, 2, 2)
    a_ref, at_ref, b_ref, c_ref, bt_ref, cc_ref, ma_ref, mb_ref = refs[:8]
    (ca_ref, cb_ref), results, (rows_of,) = refs[8:10], refs[10:-1], refs[-1:]
    pa, pb = packed_rows(ra), packed_rows(rb)
    x, y, z = here()
    ni, nj = pairs.shape[0], pairs.shape[1]
    lanes = c_ref.shape[0] // 2
    half = own_half(x, nx)
    own, other = half * lanes, (1 - half) * lanes

    for sz in range(nz):
        start = sz // 2 * (ny * ra + nx * rb)
        for sy in range(ny):
            a_ref[pl.ds(((y ^ sy) * nz + (z ^ sz)) * ra, ra), :] = packs_z[sz % 2][start : start + ra, :]
            start += ra
        for sx in range(nx):
            b_ref[pl.ds(((x ^ sx) * nz + (z ^ sz)) * rb, rb), :] = packs_z[sz % 2][start : start + rb, :]
            start += rb
    c_ref[pl.ds(own, lanes), :] = own_c[...]
    for sx in range(nx // 2):
        for sy in range(ny):
            place = ((x ^ (sx + nx // 2)) * ny + (y ^ sy)) * rc
            c_ref[pl.ds(place, rc), :] = packs_x[sx][sy * rc : (sy + 1) * rc, :]
    for n, first in enumerate((own, other)):
        at_ref[n] = a_ref[pl.ds(first, lanes), :].T
        bt_ref[n] = b_ref[pl.ds(first, lanes), :].T
    cc_ref[...] = weights(c_ref[pl.ds(other, lanes), :].T)
    gram = pair_grams(c_ref[...])
    ca_ref[...] = packed(gram, ra)
    cb_ref[...] = packed(gram, rb)
    mb_ref[...] = jnp.zeros_like(mb_ref)

    counts = [ref.shape[0] // nj for ref in own_y]

    def contract(turn, n, result):
        slices = spread(counts, turn, n)[2]
        result[...] = product(flat(pairs[pl.ds(slices, GROUP)]), cc_ref[...])

    def reduce(turn, n, result):
        part, start, first = spread(counts, turn, n)
        start = pl.multiple_of(start * nj, GROUP * nj)
        for n in range(2):
            scales = [jnp.broadcast_to(at_ref[n, pl.ds(first + g, 1), :], (TILE, lanes)) for g in range(GROUP)]
            sums = [jnp.zeros((TILE, lanes), jnp.float32)] * GROUP
            for tile in range(nj // TILE):
                rows = slice(tile * TILE, (tile + 1) * TILE)
                total = mb_ref[n, rows, :]
                across = bt_ref[n, rows, :]
                for g in range(GROUP):
                    place = g * nj + tile * TILE
                    if n == 0:
                        value = own_y[part][pl.ds(start + place, TILE), :]
                    else:
                        value = result[place : place + TILE, :]
                    total = total + scales[g] * value
                    sums[g] = sums[g] + across * value
                mb_ref[n, rows, :] = total
            for g in range(GROUP):
                ma_ref[n, pl.ds(first + g, 1), :] = jnp.sum(sums[g], axis=0, keepdims=True)

    sweep(ni // GROUP, contract, reduce, results)

    for n in range(2):
        rows_of[0, n * lanes : (n + 1) * lanes, :] = ma_ref[n].T
        rows_of[1, n * lanes : (n + 1) * lanes, :] = mb_ref[n].T
    for sz in range(nz):
        to_z = z ^ sz
        count = ny * ra + nx * rb + pa + pb
        put(
            sends[sz % 2].at[sz // 2 * count : (sz // 2 + 1) * count],
            [rows_of[0, pl.ds((((y ^ sy) * nz + to_z) * ra) ^ own, ra), :] for sy in range(ny)]
            + [rows_of[1, pl.ds((((x ^ sx) * nz + to_z) * rb) ^ own, rb), :] for sx in range(nx)]
            + [ca_ref[y * nz + to_z], cb_ref[x * nz + to_z]],
        )


def third_loop(turned, columns, weights_ref, result_refs, total_ref):
    total_ref[...] = jnp.zeros_like(total_ref)
    nk, lanes = total_ref.shape
    counts = [ref.shape[0] for ref in turned]

    def contract(turn, n, result):
        array, start, _ = spread(counts, turn, n)
        result[...] = product(flat(turned[array][pl.ds(start, GROUP)]), weights_ref[...])

    def reduce(turn, n, result):
        first = spread(counts, turn, n)[2]
        scales = [jnp.broadcast_to(columns[pl.ds(first + g, 1), :], (TILE, lanes)) for g in range(GROUP)]
        for tile in range(nk // TILE):
            rows = slice(tile * TILE, (tile + 1) * TILE)
            total = total_ref[rows, :]
            for g in range(GROUP):
                place = g * nk + tile * TILE
                total = total + scales[g] * result[place : place + TILE, :]
            total_ref[rows, :] = total

    sweep(sum(counts) // GROUP, contract, reduce, result_refs)


def partner_kernel(sizes, *refs):
    nx, ny, nz, ra, rb, rc = sizes
    (turned, (a_ref, at_ref, b_ref), sends), refs = take(refs, 3, 3, nx // 2)
    (kept_b, tb_ref, tc_ref, bb_ref, mc_ref, ba_ref, bc_ref), results, rows_of = refs[:7], refs[7:-1], refs[-1]
    x, y, z = here()
    lanes = mc_ref.shape[1]
    other = (1 - own_half(x, nx)) * lanes
    bb_ref[...] = weights(b_ref[pl.ds(other, lanes), :].T)
    gram = pair_grams(a_ref[...])
    tb_ref[...] = packed(gram, rb)
    tc_ref[...] = packed(gram, rc)
    gram = pair_grams(b_ref[...])
    ba_ref[...] = packed(gram, ra)
    bc_ref[...] = packed(gram, rc)
    third_loop(turned, at_ref.at[1], bb_ref, results, mc_ref)
    rows_of[...] = mc_ref[...].T
    for sx in range(nx // 2):
        to_x = x ^ (sx + nx // 2)
        put(
            sends[sx],
            [rows_of[pl.ds((to_x * ny + (y ^ sy)) * rc - other, rc), :] for sy in range(ny)]
            + [tb_ref[to_x * nz + z], tc_ref[to_x * ny + y]],
        )
    grams = []
    for sy in range(ny):
        grams += [ba_ref[(y ^ sy) * nz + z], bc_ref[x * ny + (y ^ sy)]]
    put(kept_b, grams)


def own_third_kernel(sizes, *refs):
    nx, ny, nz, ra, rb, rc = sizes
    (turned, (at_ref, b_ref, tb_ref, tc_ref), sends), refs = take(refs, 3, 4, nx // 2)
    (bb_ref, mc_ref), results, rows_of = refs[:2], refs[2:-1], refs[-1]
    x, y, z = here()
    lanes = mc_ref.shape[1]
    own = own_half(x, nx) * lanes
    bb_ref[...] = weights(b_ref[pl.ds(own, lanes), :].T)
    third_loop(turned, at_ref.at[0], bb_ref, results, mc_ref)
    rows_of[...] = mc_ref[...].T
    for sx in range(nx // 2):
        to_x = x ^ sx
        put(
            sends[sx],
            [rows_of[pl.ds((to_x * ny + (y ^ sy)) * rc - own, rc), :] for sy in range(ny)]
            + [tb_ref[to_x * nz + z], tc_ref[to_x * ny + y]],
        )


def core_kernel(sizes, own, other, *outs):
    count = outs[0].shape[0]
    for part, out in enumerate(outs):
        rows = slice(part * count, (part + 1) * count)
        out[...] = own[rows, :] + other[rows, :]


def middle_kernel(sizes, *refs):
    nx, ny, nz, ra, rb, rc = sizes
    (from_z, from_x, (grams_b,), for_y, for_x), (kept,) = take(refs, nz // 2, nx, 1, ny, nx)
    pa, pb, pc = packed_rows(ra), packed_rows(rb), packed_rows(rc)
    sum_z, sum_x = total_of(from_z), total_of(from_x)
    for sy in range(ny):
        put(
            for_y[sy],
            [
                sum_z[sy * ra : (sy + 1) * ra],
                sum_x[sy * rc : (sy + 1) * rc],
                grams_b[sy * (pa + pc) : (sy + 1) * (pa + pc), :],
            ],
        )
    for sx in range(nx):
        for_x[sx][...] = sum_z[ny * ra + sx * rb : ny * ra + (sx + 1) * rb]
    put(kept, [sum_z[ny * ra + nx * rb :], sum_x[ny * rc :]])


def scaled(one, other, rows, pair_weights, first_row):
    hessian = unpacked(one * other, rows)
    lane = lax.broadcasted_iota(jnp.int32, hessian.shape, 1)
    hessian = jnp.where(lane // R == lax.rem(first_row // R, 2), hessian, 0.0)
    return product(jnp.concatenate(split(hessian), axis=1), pair_weights)


def pair_weights(factor_ref, first_row):
    pair = pl.multiple_of(first_row // PAIR * PAIR, PAIR)
    return weights(factor_ref[pl.ds(pair, PAIR), :])


def grad_b_kernel(sizes, *refs):
    nx, ny, nz, ra, rb, rc = sizes
    (from_x, (kept, a_ref, b_ref, c_ref, grad_b, weights_a, weights_c)), _ = take(refs, nx, 7)
    pa, pb = packed_rows(ra), packed_rows(rb)
    x, y, z = here()
    gram_cb, gram_ab = kept[pa : pa + pb, :], kept[pa + pb : pa + 2 * pb, :]
    first = (x * nz + z) * rb
    grad_b[...] = scaled(gram_ab, gram_cb, rb, pair_weights(b_ref, first), first) - total_of(from_x)
    weights_a[...] = pair_weights(a_ref, (y * nz + z) * ra)
    weights_c[...] = pair_weights(c_ref, (x * ny + y) * rc)


def last_kernel(sizes, *refs):
    nx, ny, nz, ra, rb, rc = sizes
    (from_y, (kept, weights_a, weights_c, grad_a, grad_c)), _ = take(refs, ny, 5)
    pa, pb = packed_rows(ra), packed_rows(rb)
    x, y, z = here()
    sum_y = total_of(from_y)
    m_a, m_c = sum_y[:ra], sum_y[ra : ra + rc]
    gram_ba, gram_bc = sum_y[ra + rc : ra + rc + pa], sum_y[ra + rc + pa :]
    gram_ca, gram_ac = kept[:pa, :], kept[pa + 2 * pb :, :]
    grad_a[...] = scaled(gram_ba, gram_ca, ra, weights_a[...], (y * nz + z) * ra) - m_a
    grad_c[...] = scaled(gram_ac, gram_bc, rc, weights_c[...], (x * ny + y) * rc) - m_c


def swap(value, axis, distance):
    return lax.ppermute(value, axis, [(i, i ^ distance) for i in range(lax.axis_size(axis))])


def partners(values, axis, stride=1):
    count = lax.axis_size(axis) // stride
    if not isinstance(values, (list, tuple)):
        values = [values] * count
    return [values[0]] + [swap(values[s], axis, s * stride) for s in range(1, count)]


def swapped(value):
    return swap(value, "gz", 1)


def body(tensor, factor_a, factor_b, factor_c):
    nx, ny, nz = (lax.axis_size(name) for name in ("gx", "gy", "gz"))
    ra, rb, rc = factor_a.shape[0], factor_b.shape[0], factor_c.shape[0]
    pa, pb, pc = packed_rows(ra), packed_rows(rb), packed_rows(rc)
    lanes = factor_a.shape[1]
    total = ra * ny * nz
    sizes = (nx, ny, nz, ra, rb, rc)
    message = ny * ra + nx * rb + pa + pb
    f32, bf16 = jnp.float32, jnp.bfloat16
    vmem = pl.BlockSpec(memory_space=pltpu.VMEM)
    tensor = pltpu.with_memory_space_constraint(tensor, pltpu.VMEM)
    flops = 2 * 3 * tensor.size * total

    def rows(count):
        return jax.ShapeDtypeStruct((count, lanes), f32)

    def call(kernel, outs, args, scratch=(), limit=4, cost=None, space=pltpu.VMEM):
        return pl.pallas_call(
            lambda *refs: kernel(sizes, *refs),
            out_shape=outs,
            in_specs=[pl.BlockSpec(memory_space=space)] * len(args),
            out_specs=[vmem] * len(outs),
            scratch_shapes=scratch,
            compiler_params=pltpu.CompilerParams(vmem_limit_bytes=limit * MIB),
            cost_estimate=cost,
            name=kernel.__name__,
        )(*args)

    work = pl.CostEstimate(flops=flops, bytes_accessed=4 * tensor.size, transcendentals=0)

    ni, nj, nk = tensor.shape
    half = total // 2
    results = [pltpu.VMEM((GROUP * nj, half), f32)] * BUFFERS
    weight = pltpu.VMEM((2 * lanes, 2 * half), bf16)
    halves = pltpu.VMEM((2, lanes, half), f32)
    later = ni // 2

    def own_part(count):
        return pltpu.VMEM((count * nj, half), f32)

    def slices(count):
        return pltpu.VMEM((count, nk, 2 * nj), bf16)

    def gram_blocks(count):
        return pltpu.VMEM((total // count, packed_rows(count), PAIR), f32)

    def array(ref):
        return jax.ShapeDtypeStruct(ref.shape, ref.dtype)

    (token,) = call(token_kernel, [rows(TILE)], [], cost=work)
    (own_ac,) = call(
        own_kernel,
        [rows(ra + rc)],
        [*(pltpu.with_memory_space_constraint(value, pltpu.VMEM) for value in (factor_a, factor_c)), token],
        cost=work,
    )
    ac = partners(own_ac, "gy")
    b = partners(factor_b, "gx")
    pairs, turned_0, rows_b = call(
        tensor_kernel, [slices(ni), slices(ni // 2), rows(nx * rb)], [*b, tensor], (), 8, work
    )
    for_z, for_x = call(pack_kernel, [rows(ny * ra + nx * rb), rows(ny * rc)], [*ac, rows_b])
    from_x = partners(for_x, "gx")
    by_x = partners(for_z, "gz", 2)
    own_y_0, turned_1, own_c, weights_c = call(
        early_kernel,
        [own_part(ni - later), slices((ni - later) // 2), rows(half), array(weight)],
        [*from_x[: nx // 2], pairs],
        (),
        8,
        work,
    )
    (stack,) = call(stack_kernel, [rows(nz // 2 * (ny * ra + nx * rb))], [*by_x, own_c])
    from_z = [stack, swapped(stack)]
    own_y_1, turned_2 = call(later_kernel, [own_part(later), slices(later // 2)], [pairs, weights_c], (), 8, work)
    turned = [turned_0, turned_1, turned_2]
    own_core, other_core, block_a, columns_a, block_b, block_c = call(
        first_kernel,
        [rows(nz // 2 * message)] * 2 + [rows(total), array(halves), rows(total), rows(total)],
        [*from_z, *from_x[nx // 2 :], own_y_0, own_y_1, own_c, pairs],
        [
            halves, weight, halves, halves, gram_blocks(ra), gram_blocks(rb),
            *results, pltpu.VMEM((2, total, lanes), f32),
        ],
        12,
        work,
    )
    other_core = swapped(other_core)
    outs = call(
        partner_kernel,
        [rows(ny * rc + pb + pc)] * (nx // 2)
        + [rows(ny * (pa + pc)), array(gram_blocks(rb)), array(gram_blocks(rc))],
        [*turned, block_a, columns_a, block_b],
        [
            weight, pltpu.VMEM((nk, half), f32), gram_blocks(ra), gram_blocks(rc),
            *results, pltpu.VMEM((half, lanes), f32),
        ],
        8,
        work,
    )
    sums_x, (grams_b, grams_ab, grams_ac) = outs[: nx // 2], outs[nx // 2 :]
    sums_x = [swap(value, "gx", s + nx // 2) for s, value in enumerate(sums_x)]
    sums_z = call(core_kernel, [rows(message)] * (nz // 2), [own_core, other_core])
    sums_z = partners(sums_z, "gz", 2)
    own_x = call(
        own_third_kernel,
        [rows(ny * rc + pb + pc)] * (nx // 2),
        [*turned, columns_a, block_b, grams_ab, grams_ac],
        [weight, pltpu.VMEM((nk, half), f32), *results, pltpu.VMEM((half, lanes), f32)],
        8,
        work,
    )
    sums_x = [swap(value, "gx", s) if s else value for s, value in enumerate(own_x)] + sums_x
    outs = call(
        middle_kernel,
        [rows(ra + rc + pa + pc)] * ny + [rows(rb)] * nx + [rows(pa + pb + pb + pc)],
        [*sums_z, *sums_x, grams_b],
    )
    sums_y, sums_x, kept = outs[:ny], outs[ny : ny + nx], outs[ny + nx]
    sums_y = partners(sums_y, "gy")
    sums_x = partners(sums_x, "gx")
    pair = pltpu.VMEM((2 * PAIR, 2 * lanes), bf16)
    grad_b, weights_a, weights_c = call(
        grad_b_kernel,
        [rows(rb), array(pair), array(pair)],
        [*sums_x, kept, block_a, block_b, block_c],
        cost=work,
    )
    grad_a, grad_c = call(last_kernel, [rows(ra), rows(rc)], [*sums_y[::-1], kept, weights_a, weights_c])
    return grad_a, grad_b, grad_c


def solution(mesh):
    in_specs = (
        P("gx", "gy", "gz"),
        P(("gy", "gz"), "gx"),
        P(("gx", "gz"), "gy"),
        P(("gx", "gy"), "gz"),
    )
    out_specs = (P(("gy", "gz"), "gx"), P(("gx", "gz"), "gy"), P(("gx", "gy"), "gz"))
    return jax.shard_map(body, mesh=mesh, in_specs=in_specs, out_specs=out_specs, check_vma=False)
```
